32 devices in a mesh: parts: 2 (over x), seq: 16 (over z, y, core).
Axes of the slice: x: 2, y: 2, z: 4, core: 2. Of those that a mesh axis runs over, the one named last changes fastest.
Arguments:
- prefix: bfloat16 [64, 128, 4608], P(('parts', 'seq')), parts along dimension 0, may hold values from -6 to 6
- backbone_gain: float32 [4608], replicated, may hold values from 0.5 to 2
- kv_weight: bfloat16 [4608, 2048], P('seq'), may hold values from -8 to 8
- lengths: int32 [64], P('parts'), parts along dimension 0, may hold values from 1 to 128, as said below
- assign: int32 [64], P('parts'), parts along dimension 0, may hold values from 0 to 31, each once
- actions: float32 [64, 2, 50, 32], P(('parts', 'seq')), parts along dimension 0, may hold values from -6 to 6
- flow_noise: float32 [64, 2, 50, 32], P(('parts', 'seq')), parts along dimension 0, may hold values from -6 to 6
- timesteps: float32 [64, 2], P(('parts', 'seq')), parts along dimension 0, may hold values from 0 to 1
- expert_gain: float32 [1024], replicated, may hold values from 0.5 to 2
- action_weight: bfloat16 [32, 1024], replicated, may hold values from -1 to 1
- query_weight: bfloat16 [1024, 2048], replicated, may hold values from -0.1875 to 0.1875
- grad_attended: bfloat16 [64, 2, 50, 2048], P(('parts', 'seq')), parts along dimension 0, may hold values from -6 to 6
Outputs:
- attended: bfloat16 [64, 2, 50, 2048], P(('parts', 'seq')), parts along dimension 0
- grad_prefix: bfloat16 [64, 128, 4608], P(('parts', 'seq')), parts along dimension 0
- grad_query: bfloat16 [64, 2, 50, 2048], P(('parts', 'seq')), parts along dimension 0
The draws below stay inside these ranges and needn't reach their ends.
There are 2 independent parts, one for each index of `parts`. The reference program is written for one: setup_inputs(seed, part) draws one part's arguments, and reference() takes and returns one part's arrays. A program takes and returns all parts, laid end to end along the dimension named above; an argument that names none is the same for every part. Nothing has to cross between parts.
Inputs may be any that keep to these rules, and one draw needn't show every extreme that they name: `lengths`: some episode has length 1 and some has length 128. `assign`: a permutation; expert slot j is held by the device of seq with index j // 2.
All inputs are finite; a program needn't handle non-finite values.
Results may differ from the reference program's by a relative error of at most 0.012.
The reference program's roundings to bfloat16 on the way count: a program that leaves them out, or rounds other values in their place, can miss the bound.
Values may be sent and summed in bfloat16 or wider, within the bound.
A program may use at most 128 MiB of HBM per device.

```python
import math
import jax
import jax.numpy as jnp
from jax import lax

D = 4608
KV_HEADS = 8
Q_HEADS = 16
HEAD = 128
EXPERT_D = 1024
ACTION_DIM = 32
SPAN = 50
SAMPLES = 2
PREFIX = 128
EPISODES = 32


def draw_lengths(key, part):
    key = jax.random.fold_in(key, 11)
    first_key, second_key = jax.random.split(key)
    drawn = jax.random.randint(first_key, (EPISODES,), 1, PREFIX + 1)
    ordering = jax.random.permutation(second_key, EPISODES)
    drawn = drawn.at[ordering[0]].set(PREFIX)
    drawn = drawn.at[ordering[1]].set(1)
    return drawn.astype(jnp.int32)


def draw_kv_weight(key, part):
    key = jax.random.fold_in(key, 23)
    entry_key = jax.random.fold_in(key, 0)
    columns = 2 * KV_HEADS * HEAD
    entries = jax.random.normal(entry_key, (D, columns), jnp.float32)
    return (entries * D ** (-0.5)).astype(jnp.bfloat16)


def levels(stream_key, dims, cuts, least, top_value):
    level = 1.0
    for position, shards_of in cuts:
        steps = jax.random.uniform(jax.random.fold_in(jax.random.fold_in(stream_key, 6), position), (shards_of,), jnp.float32, least / len(cuts), top_value / len(cuts))
        level = level * jnp.repeat(jnp.exp(steps), dims[position] // shards_of).reshape((-1,) + (1,) * (len(dims) - 1 - position))
    return level


def centred(stream_key, shape, scale, bound, pieces=(), kind=jnp.bfloat16):
    gain = levels(stream_key, shape, pieces, -0.22, 0.18) if pieces else 1.0
    result = jax.random.normal(stream_key, shape, jnp.float32) * scale * gain
    return jnp.minimum(jnp.maximum(result, -bound), bound).astype(kind)


def setup_inputs(seed: int = 0, part: int = 0) -> dict:
    streams_of = jax.random.split(jax.random.key(seed), 13)
    own_keys = jax.random.split(jax.random.fold_in(streams_of[12], part), 13)
    return {
        "prefix": centred(own_keys[0], (EPISODES, PREFIX, D), 1.0, 6.0, ((0, 16),)),
        "backbone_gain": jnp.clip(jnp.exp(jax.random.uniform(streams_of[1], (D,), jnp.float32, math.log(0.5), math.log(2.0))), 0.5, 2.0),
        "kv_weight": draw_kv_weight(jax.random.fold_in(streams_of[12], 71), part),
        "lengths": draw_lengths(jax.random.fold_in(jax.random.fold_in(streams_of[12], part), 71), part),
        "assign": jax.random.permutation(own_keys[4], EPISODES).astype(jnp.int32),
        "actions": centred(own_keys[5], (EPISODES, SAMPLES, SPAN, ACTION_DIM), 1.0, 6.0, ((0, 16),), jnp.float32),
        "flow_noise": centred(own_keys[6], (EPISODES, SAMPLES, SPAN, ACTION_DIM), 1.0, 6.0, ((0, 16),), jnp.float32),
        "timesteps": jnp.clip(1.0 * jax.random.uniform(own_keys[7], (EPISODES, SAMPLES), jnp.float32) ** levels(own_keys[7], (EPISODES, SAMPLES), ((0, 16),), -0.2, 0.2), 0.0, 1.0),
        "expert_gain": jnp.clip(jnp.exp(jax.random.uniform(streams_of[8], (EXPERT_D,), jnp.float32, math.log(0.5), math.log(2.0))), 0.5, 2.0),
        "action_weight": centred(streams_of[9], (ACTION_DIM, EXPERT_D), ACTION_DIM ** -0.5, 1.0),
        "query_weight": centred(streams_of[10], (EXPERT_D, Q_HEADS * HEAD), EXPERT_D ** -0.5, 0.1875),
        "grad_attended": centred(own_keys[11], (EPISODES, SAMPLES, SPAN, Q_HEADS * HEAD), 1.0, 6.0, ((0, 16),)),
    }


def time_features(times_in, model_width):
    half_width = model_width // 2
    ladder = jnp.arange(half_width, dtype=jnp.float32)
    frequency = jnp.exp(-math.log(10000.0) * ladder / half_width)
    angles = times_in[:, None] * 1000.0 * frequency[None, :]
    return jnp.concatenate([jnp.sin(angles), jnp.cos(angles)], axis=-1)

def expert_queries(actions, flow_noise, times_in, expert_gain, action_weight, query_weight, head_dim):
    batch_count, samples, horizon, action_dim = actions.shape
    model_width = action_weight.shape[1]
    flat_times = times_in.reshape(batch_count * samples)
    mixing = flat_times[:, None, None]
    noisy_actions = mixing * flow_noise.reshape(batch_count * samples, horizon, action_dim) + (1.0 - mixing) * actions.reshape(batch_count * samples, horizon, action_dim)
    embedded = jnp.dot(noisy_actions.reshape(-1, action_dim).astype(jnp.bfloat16), action_weight, preferred_element_type=jnp.float32)
    hidden = embedded.reshape(batch_count * samples, horizon, model_width) + time_features(flat_times, model_width)[:, None, :]
    inverse_rms = lax.rsqrt(lax.optimization_barrier(jnp.mean(hidden * hidden, axis=-1, keepdims=True)) + 1e-06)
    normed = (hidden * inverse_rms * expert_gain).astype(jnp.bfloat16).reshape(-1, model_width)
    queries = (jnp.dot(normed, query_weight, preferred_element_type=jnp.float32) * head_dim ** (-0.5)).astype(jnp.bfloat16)
    return queries.reshape(batch_count, samples * horizon, query_weight.shape[1])

def attend(queries, keyval, length, upstream, kv_heads):
    batch_count, row_count, q_width = queries.shape
    positions = keyval.shape[1]
    kv_width = keyval.shape[2] // 2
    head_dim = kv_width // kv_heads
    group_size = q_width // kv_width
    score_scale = head_dim ** (-0.5)
    query_heads = queries.reshape(batch_count, row_count, kv_heads, group_size, head_dim).astype(jnp.float32)
    key_rows = keyval[:, :, :kv_width].reshape(batch_count, positions, kv_heads, head_dim).astype(jnp.float32)
    value_rows = keyval[:, :, kv_width:].reshape(batch_count, positions, kv_heads, head_dim).astype(jnp.float32)
    scores = jnp.einsum('bakgd,blkd->bkgal', query_heads, key_rows)
    visible = (jnp.arange(positions, dtype=jnp.int32)[None, :] < length[:, None])[:, None, None, None, :]
    masked = jnp.where(visible, scores, -1e+30)
    row_top = lax.optimization_barrier(jnp.max(masked, axis=-1, keepdims=True))
    exps = jnp.where(visible, jnp.exp(masked - row_top), 0.0)
    probabilities = exps / lax.optimization_barrier(jnp.sum(exps, axis=-1, keepdims=True))
    rounded = probabilities.astype(jnp.bfloat16).astype(jnp.float32)
    attended = jnp.einsum('bkgal,blkd->bakgd', rounded, value_rows).astype(jnp.bfloat16).reshape(batch_count, row_count, q_width)
    upstream_heads = upstream.reshape(batch_count, row_count, kv_heads, group_size, head_dim).astype(jnp.float32)
    grad_prob = jnp.einsum('bakgd,blkd->bkgal', upstream_heads, value_rows)
    grad_value = jnp.einsum('bkgal,bakgd->blkd', rounded, upstream_heads)
    grad_score = (probabilities * (grad_prob - lax.optimization_barrier(jnp.sum(grad_prob * probabilities, axis=-1, keepdims=True)))).astype(jnp.bfloat16).astype(jnp.float32)
    grad_query = (jnp.einsum('bkgal,blkd->bakgd', grad_score, key_rows) * score_scale).astype(jnp.bfloat16).reshape(batch_count, row_count, q_width)
    grad_key = jnp.einsum('bkgal,bakgd->blkd', grad_score, query_heads)
    grad_kv = jnp.concatenate([grad_key.reshape(batch_count, positions, kv_width), grad_value.reshape(batch_count, positions, kv_width)], axis=-1).astype(jnp.bfloat16)
    return (attended, grad_kv, grad_query)

def reference(prefix, backbone_gain, kv_weight, lengths, assign, actions, flow_noise, timesteps, expert_gain, action_weight, query_weight, grad_attended):

    def project(episode_rows):
        rows_f32 = episode_rows.astype(jnp.float32)
        inverse_rms = lax.rsqrt(lax.optimization_barrier(jnp.mean(rows_f32 * rows_f32, axis=-1, keepdims=True)) + 1e-06)
        normed = (rows_f32 * inverse_rms * backbone_gain).astype(jnp.bfloat16)
        return jnp.dot(normed, kv_weight, preferred_element_type=jnp.float32).astype(jnp.bfloat16)
    keyval = lax.map(project, prefix)
    queries = expert_queries(actions, flow_noise, timesteps, expert_gain, action_weight, query_weight, HEAD)
    upstream = grad_attended.reshape(EPISODES, SAMPLES * SPAN, Q_HEADS * HEAD)
    owned_all = keyval[assign]
    owned_len = lengths[assign]

    def single(element):
        kv_one, len_one, query_one, upstream_one = element
        outcome = attend(query_one[None], kv_one[None], len_one[None], upstream_one[None], KV_HEADS)
        return (outcome[0][0], outcome[1][0], outcome[2][0])
    attended, grad_kv, grad_query = lax.map(single, (owned_all, owned_len, queries, upstream))
    grad_keyval = jnp.zeros_like(grad_kv).at[assign].set(grad_kv)

    def backward(element):
        episode_rows, grad_rows = element
        rows_f32 = episode_rows.astype(jnp.float32)
        inverse_rms = lax.rsqrt(lax.optimization_barrier(jnp.mean(rows_f32 * rows_f32, axis=-1, keepdims=True)) + 1e-06)
        grad_normed = jnp.dot(grad_rows, kv_weight.T, preferred_element_type=jnp.float32)
        gated = grad_normed * backbone_gain
        return (inverse_rms * gated - rows_f32 * inverse_rms ** 3 * lax.optimization_barrier(jnp.mean(rows_f32 * gated, axis=-1, keepdims=True))).astype(jnp.bfloat16)
    grad_prefix = lax.map(backward, (prefix, grad_keyval))
    shape_out = (EPISODES, SAMPLES, SPAN, Q_HEADS * HEAD)
    return (attended.reshape(shape_out), grad_prefix, grad_query.reshape(shape_out))
```

```python
import math

import jax
import jax.numpy as jnp
from jax import lax
from jax.sharding import PartitionSpec as P

KV_HEADS = 8
HEAD = 128


def time_features(times_in, model_width):
    half_width = model_width // 2
    ladder = jnp.arange(half_width, dtype=jnp.float32)
    frequency = jnp.exp(-math.log(10000.0) * ladder / half_width)
    angles = times_in[:, None] * 1000.0 * frequency[None, :]
    return jnp.concatenate([jnp.sin(angles), jnp.cos(angles)], axis=-1)


def expert_queries(mixed, times_in, expert_gain, action_weight, query_weight, head_dim):
    batch_count, samples, horizon, action_dim = mixed.shape
    model_width = action_weight.shape[1]
    flat_times = times_in.reshape(batch_count * samples)
    embedded = jnp.dot(
        mixed.reshape(-1, action_dim).astype(jnp.bfloat16),
        action_weight,
        preferred_element_type=jnp.float32,
    )
    hidden = (
        embedded.reshape(batch_count * samples, horizon, model_width)
        + time_features(flat_times, model_width)[:, None, :]
    )
    inverse_rms = lax.rsqrt(jnp.mean(hidden * hidden, axis=-1, keepdims=True) + 1e-06)
    normed = (hidden * inverse_rms * expert_gain).astype(jnp.bfloat16).reshape(-1, model_width)
    queries = (
        jnp.dot(normed, query_weight, preferred_element_type=jnp.float32) * head_dim ** (-0.5)
    ).astype(jnp.bfloat16)
    return queries.reshape(batch_count, samples * horizon, query_weight.shape[1])


def attend(queries, keyval, length, upstream, kv_heads):
    batch_count, row_count, q_width = queries.shape
    positions = keyval.shape[1]
    kv_width = keyval.shape[2] // 2
    head_dim = kv_width // kv_heads
    group_size = q_width // kv_width
    score_scale = head_dim ** (-0.5)
    query_heads = queries.reshape(batch_count, row_count, kv_heads, group_size, head_dim)
    key_rows = keyval[:, :, :kv_width].reshape(batch_count, positions, kv_heads, head_dim)
    value_rows = keyval[:, :, kv_width:].reshape(batch_count, positions, kv_heads, head_dim)
    scores = jnp.einsum(
        "bakgd,blkd->bkgal", query_heads, key_rows, preferred_element_type=jnp.float32
    )
    visible = (jnp.arange(positions, dtype=jnp.int32)[None, :] < length[:, None])[
        :, None, None, None, :
    ]
    masked = jnp.where(visible, scores, -1e30)
    row_top = jnp.max(masked, axis=-1, keepdims=True)
    exps = jnp.where(visible, jnp.exp(masked - row_top), 0.0)
    probabilities = exps / jnp.sum(exps, axis=-1, keepdims=True)
    rounded = probabilities.astype(jnp.bfloat16)
    attended = (
        jnp.einsum("bkgal,blkd->bakgd", rounded, value_rows, preferred_element_type=jnp.float32)
        .astype(jnp.bfloat16)
        .reshape(batch_count, row_count, q_width)
    )
    upstream_heads = upstream.reshape(batch_count, row_count, kv_heads, group_size, head_dim)
    grad_prob = jnp.einsum(
        "bakgd,blkd->bkgal", upstream_heads, value_rows, preferred_element_type=jnp.float32
    )
    grad_value = jnp.einsum(
        "bkgal,bakgd->blkd", rounded, upstream_heads, preferred_element_type=jnp.float32
    )
    grad_score = (
        probabilities * (grad_prob - jnp.sum(grad_prob * probabilities, axis=-1, keepdims=True))
    ).astype(jnp.bfloat16)
    grad_query = (
        (
            jnp.einsum(
                "bkgal,blkd->bakgd", grad_score, key_rows, preferred_element_type=jnp.float32
            )
            * score_scale
        )
        .astype(jnp.bfloat16)
        .reshape(batch_count, row_count, q_width)
    )
    grad_key = jnp.einsum(
        "bkgal,bakgd->blkd", grad_score, query_heads, preferred_element_type=jnp.float32
    )
    grad_kv = jnp.concatenate(
        [
            grad_key.reshape(batch_count, positions, kv_width),
            grad_value.reshape(batch_count, positions, kv_width),
        ],
        axis=-1,
    ).astype(jnp.bfloat16)
    return (attended, grad_kv, grad_query)


def route_keys(block, ordering):
    spread = lax.all_to_all(block, "seq", split_axis=2, concat_axis=0, tiled=True)
    arranged = jnp.take(spread, ordering, axis=0)
    return lax.all_to_all(arranged, "seq", split_axis=0, concat_axis=2, tiled=True)


def shards(
    prefix,
    backbone_gain,
    kv_weight,
    lengths,
    assign,
    actions,
    flow_noise,
    timesteps,
    expert_gain,
    action_weight,
    query_weight,
    grad_attended,
):
    position = lax.axis_index("seq")
    owned_count, positions, model_width = prefix.shape
    episodes = assign.shape[0]
    doubled = kv_weight.shape[1]
    samples, horizon, q_width = (
        grad_attended.shape[1],
        grad_attended.shape[2],
        grad_attended.shape[3],
    )
    slot_index = jnp.arange(episodes, dtype=jnp.int32)
    matches = assign[None, :] == slot_index[:, None]
    inverse = jnp.sum(jnp.where(matches, slot_index[None, :], 0), axis=1)
    my_slots = lax.dynamic_slice_in_dim(inverse, position * owned_count, owned_count)
    owned_len = lax.dynamic_slice_in_dim(lengths, position * owned_count, owned_count)

    mixing = timesteps[:, :, None, None]
    mixed = mixing * flow_noise + (1.0 - mixing) * actions
    packed = jnp.concatenate(
        [mixed.reshape(owned_count, -1), timesteps], axis=1
    )
    gathered = lax.all_gather(packed, "seq", axis=0, tiled=True)
    own_packed = jnp.take(gathered, my_slots, axis=0)
    whole_weight = lax.all_gather(kv_weight, "seq", axis=0, tiled=True)
    upstream = route_keys(
        grad_attended.reshape(owned_count, samples * horizon, q_width), inverse
    )
    own_mixed = own_packed[:, :-samples].reshape(owned_count, samples, horizon, -1)
    queries = expert_queries(
        own_mixed, own_packed[:, -samples:], expert_gain, action_weight, query_weight, HEAD
    )

    prefix_f32 = prefix.astype(jnp.float32)
    inverse_rms = lax.rsqrt(jnp.mean(prefix_f32 * prefix_f32, axis=-1, keepdims=True) + 1e-06)
    normed = (
        (prefix_f32 * inverse_rms * backbone_gain)
        .astype(jnp.bfloat16)
        .reshape(owned_count * positions, model_width)
    )
    product = jnp.dot(normed, whole_weight, preferred_element_type=jnp.float32)
    keyval = product.astype(jnp.bfloat16).reshape(owned_count, positions, doubled)
    attended, grad_kv, grad_query = attend(queries, keyval, owned_len, upstream, KV_HEADS)
    attended = route_keys(attended, assign)
    grad_query = route_keys(grad_query, assign)
    restored = grad_kv.reshape(owned_count * positions, doubled)
    grad_normed = lax.dot_general(
        restored, whole_weight, (((1,), (1,)), ((), ())), preferred_element_type=jnp.float32
    )
    gated = grad_normed.reshape(owned_count, positions, model_width) * backbone_gain
    grad_prefix = (
        inverse_rms * gated
        - prefix_f32 * inverse_rms**3 * jnp.mean(prefix_f32 * gated, axis=-1, keepdims=True)
    ).astype(jnp.bfloat16)
    shape_out = (owned_count, samples, horizon, q_width)
    return (attended.reshape(shape_out), grad_prefix, grad_query.reshape(shape_out))


def solution(mesh):
    placed = (
        P(("parts", "seq"), None, None),
        P(),
        P("seq", None),
        P("parts"),
        P("parts"),
        P(("parts", "seq"), None, None, None),
        P(("parts", "seq"), None, None, None),
        P(("parts", "seq"), None),
        P(),
        P(),
        P(),
        P(("parts", "seq"), None, None, None),
    )
    return jax.shard_map(
        shards,
        mesh=mesh,
        in_specs=placed,
        out_specs=(
            P(("parts", "seq"), None, None, None),
            P(("parts", "seq"), None, None),
            P(("parts", "seq"), None, None, None),
        ),
        check_vma=False,
    )
```

```python
import functools
import math

import jax
import jax.numpy as jnp
from jax import lax
from jax.experimental import pallas as pl
from jax.experimental.pallas import tpu as pltpu
from jax.sharding import PartitionSpec as P

KV_HEADS = 8
HEAD = 128


def time_features(times_in, model_width):
    half_width = model_width // 2
    ladder = jnp.arange(half_width, dtype=jnp.float32)
    frequency = jnp.exp(-math.log(10000.0) * ladder / half_width)
    angles = times_in[:, None] * 1000.0 * frequency[None, :]
    return jnp.concatenate([jnp.sin(angles), jnp.cos(angles)], axis=-1)


def expert_queries(
    actions, flow_noise, times_in, expert_gain, action_weight, query_weight, head_dim
):
    batch_count, samples, horizon, action_dim = actions.shape
    model_width = action_weight.shape[1]
    flat_times = times_in.reshape(batch_count * samples)
    mixing = flat_times[:, None, None]
    noisy_actions = mixing * flow_noise.reshape(batch_count * samples, horizon, action_dim) + (
        1.0 - mixing
    ) * actions.reshape(batch_count * samples, horizon, action_dim)
    embedded = jnp.dot(
        noisy_actions.reshape(-1, action_dim).astype(jnp.bfloat16),
        action_weight,
        preferred_element_type=jnp.float32,
    )
    hidden = (
        embedded.reshape(batch_count * samples, horizon, model_width)
        + time_features(flat_times, model_width)[:, None, :]
    )
    inverse_rms = lax.rsqrt(jnp.mean(hidden * hidden, axis=-1, keepdims=True) + 1e-06)
    normed = (hidden * inverse_rms * expert_gain).astype(jnp.bfloat16).reshape(-1, model_width)
    queries = (
        jnp.dot(normed, query_weight, preferred_element_type=jnp.float32) * head_dim ** (-0.5)
    ).astype(jnp.bfloat16)
    return queries.reshape(batch_count, samples * horizon, query_weight.shape[1])


def attend(queries, keyval, length, upstream, kv_heads):
    batch_count, row_count, q_width = queries.shape
    positions = keyval.shape[1]
    kv_width = keyval.shape[2] // 2
    head_dim = kv_width // kv_heads
    group_size = q_width // kv_width
    score_scale = head_dim ** (-0.5)
    query_heads = queries.reshape(batch_count, row_count, kv_heads, group_size, head_dim)
    key_rows = keyval[:, :, :kv_width].reshape(batch_count, positions, kv_heads, head_dim)
    value_rows = keyval[:, :, kv_width:].reshape(batch_count, positions, kv_heads, head_dim)
    scores = jnp.einsum(
        "bakgd,blkd->bkgal", query_heads, key_rows, preferred_element_type=jnp.float32
    )
    visible = (jnp.arange(positions, dtype=jnp.int32)[None, :] < length[:, None])[
        :, None, None, None, :
    ]
    masked = jnp.where(visible, scores, -1e30)
    row_top = jnp.max(masked, axis=-1, keepdims=True)
    exps = jnp.where(visible, jnp.exp(masked - row_top), 0.0)
    probabilities = exps / jnp.sum(exps, axis=-1, keepdims=True)
    rounded = probabilities.astype(jnp.bfloat16)
    attended = (
        jnp.einsum("bkgal,blkd->bakgd", rounded, value_rows, preferred_element_type=jnp.float32)
        .astype(jnp.bfloat16)
        .reshape(batch_count, row_count, q_width)
    )
    upstream_heads = upstream.reshape(batch_count, row_count, kv_heads, group_size, head_dim)
    grad_prob = jnp.einsum(
        "bakgd,blkd->bkgal", upstream_heads, value_rows, preferred_element_type=jnp.float32
    )
    grad_value = jnp.einsum(
        "bkgal,bakgd->blkd", rounded, upstream_heads, preferred_element_type=jnp.float32
    )
    grad_score = (
        probabilities * (grad_prob - jnp.sum(grad_prob * probabilities, axis=-1, keepdims=True))
    ).astype(jnp.bfloat16)
    grad_query = (
        (
            jnp.einsum(
                "bkgal,blkd->bakgd", grad_score, key_rows, preferred_element_type=jnp.float32
            )
            * score_scale
        )
        .astype(jnp.bfloat16)
        .reshape(batch_count, row_count, q_width)
    )
    grad_key = jnp.einsum(
        "bkgal,bakgd->blkd", grad_score, query_heads, preferred_element_type=jnp.float32
    )
    grad_kv = jnp.concatenate(
        [
            grad_key.reshape(batch_count, positions, kv_width),
            grad_value.reshape(batch_count, positions, kv_width),
        ],
        axis=-1,
    ).astype(jnp.bfloat16)
    return (attended, grad_kv, grad_query)


def route_keys(block, ordering):
    spread = lax.all_to_all(block, "seq", split_axis=2, concat_axis=0, tiled=True)
    arranged = jnp.take(spread, ordering, axis=0)
    return lax.all_to_all(arranged, "seq", split_axis=0, concat_axis=2, tiled=True)


def exchange_kernel(
    n,
    order_ref,
    inverse_ref,
    length_ref,
    keyval_ref,
    query_ref,
    upstream_ref,
    attended_ref,
    grad_query_ref,
    restored_ref,
    owned,
    spread,
    arranged,
    grads,
    spread_back,
    arranged_back,
    send_sems,
    recv_sems,
    local_sems,
):
    me = lax.axis_index("seq")
    own = keyval_ref.shape[0]
    heads = KV_HEADS
    episodes = spread.shape[0]

    def columns(index):
        return pl.ds(pl.multiple_of(index * HEAD, HEAD), HEAD)

    def rows(index):
        return pl.ds(index * own, own)

    def remote(stage, source, target, device, origin):
        return pltpu.make_async_remote_copy(
            src_ref=source,
            dst_ref=target,
            send_sem=send_sems.at[stage, device],
            recv_sem=recv_sems.at[stage, origin],
            device_id={"seq": device},
            device_id_type=pl.DeviceIdType.MESH,
        )

    def others(body):
        def step(k, carry):
            body(lax.rem(me + k, n))
            return carry

        lax.fori_loop(1, n, step, 0)

    barrier = pltpu.get_barrier_semaphore()
    others(
        lambda d: pl.semaphore_signal(
            barrier, inc=1, device_id={"seq": d}, device_id_type=pl.DeviceIdType.MESH
        )
    )
    pl.semaphore_wait(barrier, n - 1)

    def first(d):
        return remote(0, keyval_ref.at[:, :, columns(d)], spread.at[rows(me)], d, me)

    def first_in(d):
        return remote(0, keyval_ref.at[:, :, columns(d)], spread.at[rows(d)], d, d)

    kept = pltpu.make_async_copy(
        keyval_ref.at[:, :, columns(me)], spread.at[rows(me)], local_sems.at[0]
    )
    kept.start()
    others(lambda d: first(d).start())
    kept.wait()
    others(lambda d: first_in(d).wait_recv())

    def arrange(source, target, order):
        def step(e, carry):
            target[e] = source[order[e]]
            return carry

        lax.fori_loop(0, episodes, step, 0)

    arrange(spread, arranged, order_ref)

    def second(d):
        return remote(1, arranged.at[rows(d)], owned.at[:, :, columns(me)], d, me)

    def second_in(d):
        return remote(1, arranged.at[rows(d)], owned.at[:, :, columns(d)], d, d)

    kept = pltpu.make_async_copy(
        arranged.at[rows(me)], owned.at[:, :, columns(me)], local_sems.at[1]
    )
    kept.start()
    others(lambda d: second(d).start())
    kept.wait()

    def third(d):
        return remote(2, grads.at[:, :, columns(d)], spread_back.at[rows(me)], d, me)

    def third_in(d):
        return remote(2, grads.at[:, :, columns(d)], spread_back.at[rows(d)], d, d)

    def head(h, carry):
        for d in (h, h + heads):
            @pl.when(d != me)
            def _():
                second_in(d).wait_recv()

        even, odd = columns(2 * h), columns(2 * h + 1)
        for s in range(own):
            keys = owned[s, :, columns(h)]
            values = owned[s, :, columns(h + heads)]
            query = jnp.concatenate([query_ref[s, :, even], query_ref[s, :, odd]], axis=0)
            upstream = jnp.concatenate(
                [upstream_ref[s, :, even], upstream_ref[s, :, odd]], axis=0
            )
            half = query.shape[0] // 2
            scores = lax.dot_general(
                query, keys, (((1,), (1,)), ((), ())), preferred_element_type=jnp.float32
            )
            visible = lax.broadcasted_iota(jnp.int32, scores.shape, 1) < length_ref[s]
            masked = jnp.where(visible, scores, -1e30)
            exps = jnp.where(
                visible, jnp.exp(masked - jnp.max(masked, axis=-1, keepdims=True)), 0.0
            )
            probabilities = exps / jnp.sum(exps, axis=-1, keepdims=True)
            rounded = probabilities.astype(jnp.bfloat16)
            attended = jnp.dot(rounded, values, preferred_element_type=jnp.float32)
            grad_prob = lax.dot_general(
                upstream, values, (((1,), (1,)), ((), ())), preferred_element_type=jnp.float32
            )
            grad_value = lax.dot_general(
                rounded, upstream, (((0,), (0,)), ((), ())), preferred_element_type=jnp.float32
            )
            grad_score = (
                probabilities
                * (grad_prob - jnp.sum(grad_prob * probabilities, axis=-1, keepdims=True))
            ).astype(jnp.bfloat16)
            grad_query = (
                jnp.dot(grad_score, keys, preferred_element_type=jnp.float32) * HEAD ** (-0.5)
            )
            grad_key = lax.dot_general(
                grad_score, query, (((0,), (0,)), ((), ())), preferred_element_type=jnp.float32
            )
            attended_ref[s, :, even] = attended[:half].astype(jnp.bfloat16)
            attended_ref[s, :, odd] = attended[half:].astype(jnp.bfloat16)
            grad_query_ref[s, :, even] = grad_query[:half].astype(jnp.bfloat16)
            grad_query_ref[s, :, odd] = grad_query[half:].astype(jnp.bfloat16)
            grads[s, :, columns(h)] = grad_key.astype(jnp.bfloat16)
            grads[s, :, columns(h + heads)] = grad_value.astype(jnp.bfloat16)
        for d in (h, h + heads):
            @pl.when(d != me)
            def _():
                third(d).start()
        return carry

    lax.fori_loop(0, heads, head, 0)

    kept = pltpu.make_async_copy(
        grads.at[:, :, columns(me)], spread_back.at[rows(me)], local_sems.at[2]
    )
    kept.start()
    kept.wait()
    others(lambda d: third_in(d).wait_recv())
    arrange(spread_back, arranged_back, inverse_ref)

    def fourth(d):
        return remote(3, arranged_back.at[rows(d)], restored_ref.at[:, :, columns(me)], d, me)

    def fourth_in(d):
        return remote(3, arranged_back.at[rows(d)], restored_ref.at[:, :, columns(d)], d, d)

    kept = pltpu.make_async_copy(
        arranged_back.at[rows(me)], restored_ref.at[:, :, columns(me)], local_sems.at[3]
    )
    kept.start()
    others(lambda d: fourth(d).start())
    kept.wait()
    others(lambda d: fourth_in(d).wait_recv())

    def sent(d):
        first(d).wait_send()
        second(d).wait_send()
        third(d).wait_send()
        fourth(d).wait_send()

    others(sent)


def exchange(assign, inverse, owned_len, keyval, queries, upstream):
    n = lax.axis_size("seq")
    owned_count, positions, doubled = keyval.shape
    episodes = assign.shape[0]
    padded = jax.ShapeDtypeStruct(queries.shape, jnp.bfloat16)
    blocks = pltpu.VMEM((episodes, positions, HEAD), jnp.bfloat16)
    whole = pltpu.VMEM(keyval.shape, jnp.bfloat16)
    memory = pl.BlockSpec(memory_space=pltpu.VMEM)
    scalars = pl.BlockSpec(memory_space=pltpu.SMEM)
    return pl.pallas_call(
        functools.partial(exchange_kernel, n),
        out_shape=(padded, padded, jax.ShapeDtypeStruct(keyval.shape, jnp.bfloat16)),
        in_specs=[scalars] * 3 + [memory] * 3,
        out_specs=(memory,) * 3,
        scratch_shapes=[
            whole,
            blocks,
            blocks,
            whole,
            blocks,
            blocks,
            pltpu.SemaphoreType.DMA((4, n)),
            pltpu.SemaphoreType.DMA((4, n)),
            pltpu.SemaphoreType.DMA((4,)),
        ],
        compiler_params=pltpu.CompilerParams(
            collective_id=0, has_side_effects=True, vmem_limit_bytes=40 * 2**20
        ),
        name="exchange",
    )(assign, inverse, owned_len, keyval, queries, upstream)


def shards(
    prefix,
    backbone_gain,
    kv_weight,
    lengths,
    assign,
    actions,
    flow_noise,
    timesteps,
    expert_gain,
    action_weight,
    query_weight,
    grad_attended,
):
    position = lax.axis_index("seq")
    owned_count, positions, model_width = prefix.shape
    episodes = assign.shape[0]
    doubled = kv_weight.shape[1]
    samples, horizon, q_width = (
        grad_attended.shape[1],
        grad_attended.shape[2],
        grad_attended.shape[3],
    )
    prefix_f32 = prefix.astype(jnp.float32)
    inverse_rms = lax.rsqrt(jnp.mean(prefix_f32 * prefix_f32, axis=-1, keepdims=True) + 1e-06)
    normed = (
        (prefix_f32 * inverse_rms * backbone_gain)
        .astype(jnp.bfloat16)
        .reshape(owned_count * positions, model_width)
    )
    whole_weight = lax.all_gather(kv_weight, "seq", axis=0, tiled=True)
    product = jnp.dot(normed, whole_weight, preferred_element_type=jnp.float32)
    keyval = product.astype(jnp.bfloat16).reshape(owned_count, positions, doubled)
    queries = expert_queries(
        actions, flow_noise, timesteps, expert_gain, action_weight, query_weight, HEAD
    )
    upstream = grad_attended.reshape(owned_count, samples * horizon, q_width)
    slot_index = jnp.arange(episodes, dtype=jnp.int32)
    matches = assign[None, :] == slot_index[:, None]
    inverse = jnp.sum(jnp.where(matches, slot_index[None, :], 0), axis=1)
    my_slots = lax.dynamic_slice_in_dim(assign, position * owned_count, owned_count)
    chosen = slot_index[None, :] == my_slots[:, None]
    owned_len = jnp.sum(jnp.where(chosen, lengths[None, :], 0), axis=1)
    if doubled // lax.axis_size("seq") == HEAD:
        row_count = samples * horizon
        extra = ((0, 0), (0, positions - row_count), (0, 0))
        attended, grad_query, grad_keyval = exchange(
            assign, inverse, owned_len, keyval, jnp.pad(queries, extra), jnp.pad(upstream, extra)
        )
        attended, grad_query = attended[:, :row_count], grad_query[:, :row_count]
    else:
        owned_kv = route_keys(keyval, assign)
        attended, grad_kv, grad_query = attend(queries, owned_kv, owned_len, upstream, KV_HEADS)
        grad_keyval = route_keys(grad_kv, inverse)
    restored = grad_keyval.reshape(owned_count * positions, doubled)
    grad_normed = lax.dot_general(
        restored, whole_weight, (((1,), (1,)), ((), ())), preferred_element_type=jnp.float32
    )
    gated = grad_normed.reshape(owned_count, positions, model_width) * backbone_gain
    grad_prefix = (
        inverse_rms * gated
        - prefix_f32 * inverse_rms**3 * jnp.mean(prefix_f32 * gated, axis=-1, keepdims=True)
    ).astype(jnp.bfloat16)
    shape_out = (owned_count, samples, horizon, q_width)
    return (attended.reshape(shape_out), grad_prefix, grad_query.reshape(shape_out))


def solution(mesh):
    placed = (
        P(("parts", "seq"), None, None),
        P(),
        P("seq", None),
        P("parts"),
        P("parts"),
        P(("parts", "seq"), None, None, None),
        P(("parts", "seq"), None, None, None),
        P(("parts", "seq"), None),
        P(),
        P(),
        P(),
        P(("parts", "seq"), None, None, None),
    )
    return jax.shard_map(
        shards,
        mesh=mesh,
        in_specs=placed,
        out_specs=(
            P(("parts", "seq"), None, None, None),
            P(("parts", "seq"), None, None),
            P(("parts", "seq"), None, None, None),
        ),
        check_vma=False,
    )
```

```python
import functools
import math

import jax
import jax.numpy as jnp
from jax import lax
from jax.experimental import pallas as pl
from jax.experimental.pallas import tpu as pltpu
from jax.sharding import PartitionSpec as P

KV_HEADS = 8
HEAD = 128


def time_features(times_in, model_width):
    half_width = model_width // 2
    ladder = jnp.arange(half_width, dtype=jnp.float32)
    frequency = jnp.exp(-math.log(10000.0) * ladder / half_width)
    angles = times_in[:, None] * 1000.0 * frequency[None, :]
    return jnp.concatenate([jnp.sin(angles), jnp.cos(angles)], axis=-1)


def expert_queries(
    actions, flow_noise, times_in, expert_gain, action_weight, query_weight, head_dim
):
    batch_count, samples, horizon, action_dim = actions.shape
    model_width = action_weight.shape[1]
    flat_times = times_in.reshape(batch_count * samples)
    mixing = flat_times[:, None, None]
    noisy_actions = mixing * flow_noise.reshape(batch_count * samples, horizon, action_dim) + (
        1.0 - mixing
    ) * actions.reshape(batch_count * samples, horizon, action_dim)
    embedded = jnp.dot(
        noisy_actions.reshape(-1, action_dim).astype(jnp.bfloat16),
        action_weight,
        preferred_element_type=jnp.float32,
    )
    hidden = (
        embedded.reshape(batch_count * samples, horizon, model_width)
        + time_features(flat_times, model_width)[:, None, :]
    )
    inverse_rms = lax.rsqrt(jnp.mean(hidden * hidden, axis=-1, keepdims=True) + 1e-06)
    normed = (hidden * inverse_rms * expert_gain).astype(jnp.bfloat16).reshape(-1, model_width)
    queries = (
        jnp.dot(normed, query_weight, preferred_element_type=jnp.float32) * head_dim ** (-0.5)
    ).astype(jnp.bfloat16)
    return queries.reshape(batch_count, samples * horizon, query_weight.shape[1])


def attend(queries, keyval, length, upstream, kv_heads):
    batch_count, row_count, q_width = queries.shape
    positions = keyval.shape[1]
    kv_width = keyval.shape[2] // 2
    head_dim = kv_width // kv_heads
    group_size = q_width // kv_width
    score_scale = head_dim ** (-0.5)
    query_heads = queries.reshape(batch_count, row_count, kv_heads, group_size, head_dim)
    key_rows = keyval[:, :, :kv_width].reshape(batch_count, positions, kv_heads, head_dim)
    value_rows = keyval[:, :, kv_width:].reshape(batch_count, positions, kv_heads, head_dim)
    scores = jnp.einsum(
        "bakgd,blkd->bkgal", query_heads, key_rows, preferred_element_type=jnp.float32
    )
    visible = (jnp.arange(positions, dtype=jnp.int32)[None, :] < length[:, None])[
        :, None, None, None, :
    ]
    masked = jnp.where(visible, scores, -1e30)
    row_top = jnp.max(masked, axis=-1, keepdims=True)
    exps = jnp.where(visible, jnp.exp(masked - row_top), 0.0)
    probabilities = exps / jnp.sum(exps, axis=-1, keepdims=True)
    rounded = probabilities.astype(jnp.bfloat16)
    attended = (
        jnp.einsum("bkgal,blkd->bakgd", rounded, value_rows, preferred_element_type=jnp.float32)
        .astype(jnp.bfloat16)
        .reshape(batch_count, row_count, q_width)
    )
    upstream_heads = upstream.reshape(batch_count, row_count, kv_heads, group_size, head_dim)
    grad_prob = jnp.einsum(
        "bakgd,blkd->bkgal", upstream_heads, value_rows, preferred_element_type=jnp.float32
    )
    grad_value = jnp.einsum(
        "bkgal,bakgd->blkd", rounded, upstream_heads, preferred_element_type=jnp.float32
    )
    grad_score = (
        probabilities * (grad_prob - jnp.sum(grad_prob * probabilities, axis=-1, keepdims=True))
    ).astype(jnp.bfloat16)
    grad_query = (
        (
            jnp.einsum(
                "bkgal,blkd->bakgd", grad_score, key_rows, preferred_element_type=jnp.float32
            )
            * score_scale
        )
        .astype(jnp.bfloat16)
        .reshape(batch_count, row_count, q_width)
    )
    grad_key = jnp.einsum(
        "bkgal,bakgd->blkd", grad_score, query_heads, preferred_element_type=jnp.float32
    )
    grad_kv = jnp.concatenate(
        [
            grad_key.reshape(batch_count, positions, kv_width),
            grad_value.reshape(batch_count, positions, kv_width),
        ],
        axis=-1,
    ).astype(jnp.bfloat16)
    return (attended, grad_kv, grad_query)


def route_keys(block, ordering):
    spread = lax.all_to_all(block, "seq", split_axis=2, concat_axis=0, tiled=True)
    arranged = jnp.take(spread, ordering, axis=0)
    return lax.all_to_all(arranged, "seq", split_axis=0, concat_axis=2, tiled=True)


def exchange_kernel(
    n,
    order_ref,
    inverse_ref,
    length_ref,
    keyval_ref,
    query_ref,
    upstream_ref,
    attended_ref,
    grad_query_ref,
    restored_ref,
    owned,
    spread,
    arranged,
    grads,
    spread_back,
    arranged_back,
    send_sems,
    recv_sems,
    local_sems,
):
    me = lax.axis_index("seq")
    own = keyval_ref.shape[0]
    heads = KV_HEADS
    episodes = spread.shape[0]

    def columns(index):
        return pl.ds(pl.multiple_of(index * HEAD, HEAD), HEAD)

    def rows(index):
        return pl.ds(index * own, own)

    def remote(stage, source, target, device, origin):
        return pltpu.make_async_remote_copy(
            src_ref=source,
            dst_ref=target,
            send_sem=send_sems.at[stage, device],
            recv_sem=recv_sems.at[stage, origin],
            device_id={"seq": device},
            device_id_type=pl.DeviceIdType.MESH,
        )

    def others(body):
        def step(k, carry):
            body(lax.rem(me + k, n))
            return carry

        lax.fori_loop(1, n, step, 0)

    barrier = pltpu.get_barrier_semaphore()
    others(
        lambda d: pl.semaphore_signal(
            barrier, inc=1, device_id={"seq": d}, device_id_type=pl.DeviceIdType.MESH
        )
    )
    pl.semaphore_wait(barrier, n - 1)

    def first(d):
        return remote(0, keyval_ref.at[:, :, columns(d)], spread.at[rows(me)], d, me)

    def first_in(d):
        return remote(0, keyval_ref.at[:, :, columns(d)], spread.at[rows(d)], d, d)

    kept = pltpu.make_async_copy(
        keyval_ref.at[:, :, columns(me)], spread.at[rows(me)], local_sems.at[0]
    )
    kept.start()
    others(lambda d: first(d).start())
    kept.wait()
    others(lambda d: first_in(d).wait_recv())

    def arrange(source, target, order):
        def step(e, carry):
            target[e] = source[order[e]]
            return carry

        lax.fori_loop(0, episodes, step, 0)

    arrange(spread, arranged, order_ref)

    def second(d):
        return remote(1, arranged.at[rows(d)], owned.at[:, :, columns(me)], d, me)

    def second_in(d):
        return remote(1, arranged.at[rows(d)], owned.at[:, :, columns(d)], d, d)

    kept = pltpu.make_async_copy(
        arranged.at[rows(me)], owned.at[:, :, columns(me)], local_sems.at[1]
    )
    kept.start()
    others(lambda d: second(d).start())
    kept.wait()

    def third(d):
        return remote(2, grads.at[:, :, columns(d)], spread_back.at[rows(me)], d, me)

    def third_in(d):
        return remote(2, grads.at[:, :, columns(d)], spread_back.at[rows(d)], d, d)

    def head(h, carry):
        for d in (h, h + heads):
            @pl.when(d != me)
            def _():
                second_in(d).wait_recv()

        even, odd = columns(2 * h), columns(2 * h + 1)
        for s in range(own):
            keys = owned[s, :, columns(h)]
            values = owned[s, :, columns(h + heads)]
            query = jnp.concatenate([query_ref[s, :, even], query_ref[s, :, odd]], axis=0)
            upstream = jnp.concatenate(
                [upstream_ref[s, :, even], upstream_ref[s, :, odd]], axis=0
            )
            half = query.shape[0] // 2
            scores = lax.dot_general(
                query, keys, (((1,), (1,)), ((), ())), preferred_element_type=jnp.float32
            )
            visible = lax.broadcasted_iota(jnp.int32, scores.shape, 1) < length_ref[s]
            masked = jnp.where(visible, scores, -1e30)
            exps = jnp.where(
                visible, jnp.exp(masked - jnp.max(masked, axis=-1, keepdims=True)), 0.0
            )
            probabilities = exps / jnp.sum(exps, axis=-1, keepdims=True)
            rounded = probabilities.astype(jnp.bfloat16)
            attended = jnp.dot(rounded, values, preferred_element_type=jnp.float32)
            grad_prob = lax.dot_general(
                upstream, values, (((1,), (1,)), ((), ())), preferred_element_type=jnp.float32
            )
            grad_value = lax.dot_general(
                rounded, upstream, (((0,), (0,)), ((), ())), preferred_element_type=jnp.float32
            )
            grad_score = (
                probabilities
                * (grad_prob - jnp.sum(grad_prob * probabilities, axis=-1, keepdims=True))
            ).astype(jnp.bfloat16)
            grad_query = (
                jnp.dot(grad_score, keys, preferred_element_type=jnp.float32) * HEAD ** (-0.5)
            )
            grad_key = lax.dot_general(
                grad_score, query, (((0,), (0,)), ((), ())), preferred_element_type=jnp.float32
            )
            attended_ref[s, :, even] = attended[:half].astype(jnp.bfloat16)
            attended_ref[s, :, odd] = attended[half:].astype(jnp.bfloat16)
            grad_query_ref[s, :, even] = grad_query[:half].astype(jnp.bfloat16)
            grad_query_ref[s, :, odd] = grad_query[half:].astype(jnp.bfloat16)
            grads[s, :, columns(h)] = grad_key.astype(jnp.bfloat16)
            grads[s, :, columns(h + heads)] = grad_value.astype(jnp.bfloat16)
        for d in (h, h + heads):
            @pl.when(d != me)
            def _():
                third(d).start()
        return carry

    lax.fori_loop(0, heads, head, 0)

    kept = pltpu.make_async_copy(
        grads.at[:, :, columns(me)], spread_back.at[rows(me)], local_sems.at[2]
    )
    kept.start()
    kept.wait()
    others(lambda d: third_in(d).wait_recv())
    arrange(spread_back, arranged_back, inverse_ref)

    def fourth(d):
        return remote(3, arranged_back.at[rows(d)], restored_ref.at[:, :, columns(me)], d, me)

    def fourth_in(d):
        return remote(3, arranged_back.at[rows(d)], restored_ref.at[:, :, columns(d)], d, d)

    kept = pltpu.make_async_copy(
        arranged_back.at[rows(me)], restored_ref.at[:, :, columns(me)], local_sems.at[3]
    )
    kept.start()
    others(lambda d: fourth(d).start())
    kept.wait()
    others(lambda d: fourth_in(d).wait_recv())

    def sent(d):
        first(d).wait_send()
        second(d).wait_send()
        third(d).wait_send()
        fourth(d).wait_send()

    others(sent)


def exchange(assign, inverse, owned_len, keyval, queries, upstream):
    n = lax.axis_size("seq")
    owned_count, positions, doubled = keyval.shape
    episodes = assign.shape[0]
    padded = jax.ShapeDtypeStruct(queries.shape, jnp.bfloat16)
    blocks = pltpu.VMEM((episodes, positions, HEAD), jnp.bfloat16)
    whole = pltpu.VMEM(keyval.shape, jnp.bfloat16)
    memory = pl.BlockSpec(memory_space=pltpu.VMEM)
    scalars = pl.BlockSpec(memory_space=pltpu.SMEM)
    return pl.pallas_call(
        functools.partial(exchange_kernel, n),
        out_shape=(padded, padded, jax.ShapeDtypeStruct(keyval.shape, jnp.bfloat16)),
        in_specs=[scalars] * 3 + [memory] * 3,
        out_specs=(memory,) * 3,
        scratch_shapes=[
            whole,
            blocks,
            blocks,
            whole,
            blocks,
            blocks,
            pltpu.SemaphoreType.DMA((4, n)),
            pltpu.SemaphoreType.DMA((4, n)),
            pltpu.SemaphoreType.DMA((4,)),
        ],
        compiler_params=pltpu.CompilerParams(
            collective_id=0, has_side_effects=True, vmem_limit_bytes=40 * 2**20
        ),
        name="exchange",
    )(assign, inverse, owned_len, keyval, queries, upstream)


def gather_kernel(
    n,
    weight_ref,
    normed_ref,
    whole_ref,
    keyval_ref,
    held,
    total,
    ring_send,
    ring_recv,
    pair_send,
    pair_recv,
    cross_send,
    cross_recv,
    start_send,
    start_recv,
    out_sems,
):
    chips = n // 2
    part = lax.axis_index("parts")
    me = lax.axis_index("seq")
    chip, core = me // 2, lax.rem(me, 2)
    depth_place, side = chip // 2, lax.rem(chip, 2)
    place = depth_place + side * (chips - 1 - 2 * depth_place)
    width = held.shape[2]
    quarter, half, piece = width // 4, width // 2, width // 16

    def chip_at(position):
        position = lax.rem(position + 2 * chips, chips)
        return jnp.where(position < chips // 2, 2 * position, 2 * (chips - 1 - position) + 1)

    def span(start, size):
        return pl.ds(pl.multiple_of(start, piece), size)

    def columns(which, kind):
        if kind == 0:
            return span(which * quarter, 2 * piece)
        own = part if kind == 1 else 1 - part
        return span(which * quarter + (2 + own) * piece, piece)

    def rows(of):
        return pl.ds(of * 2, 2)

    def arriving(d, s):
        return chip_at(place - 1 - s if d == 0 else place + 1 + s)

    def leaving(d, s):
        return chip_at(place - s if d == 0 else place + s)

    def send(ref, device, send_sem, recv_sem):
        return pltpu.make_async_remote_copy(
            src_ref=ref,
            dst_ref=ref,
            send_sem=send_sem,
            recv_sem=recv_sem,
            device_id=device,
            device_id_type=pl.DeviceIdType.MESH,
        )

    onward = [{"seq": chip_at(place + 1) * 2 + core}, {"seq": chip_at(place - 1) * 2 + core}]
    sibling = {"seq": chip * 2 + 1 - core}
    opposite = {"parts": 1 - part, "seq": me}

    def ring(d, kind, s, of):
        ref = held.at[rows(of), :, columns(core * 2 + d, kind)]
        return send(ref, onward[d], ring_send.at[d, kind, s], ring_recv.at[d, kind, s])

    def pair(d, kind, s, whose):
        ref = held.at[rows(arriving(d, s)), :, columns(whose * 2 + d, kind)]
        return send(ref, sibling, pair_send.at[d, kind, s], pair_recv.at[d, kind, s])

    def cross(d, kind, s):
        ref = held.at[rows(arriving(d, s)), :, columns(core * 2 + d, kind)]
        return send(ref, opposite, cross_send.at[d, s], cross_recv.at[d, s])

    def start(k, shard, whose):
        ref = held.at[shard, :, span(whose * half, half)]
        return send(ref, sibling, start_send.at[k], start_recv.at[k])

    barrier = pltpu.get_barrier_semaphore()
    for device in (*onward, sibling, opposite):
        pl.semaphore_signal(
            barrier, inc=1, device_id=device, device_id_type=pl.DeviceIdType.MESH
        )
    mine = pltpu.make_async_copy(weight_ref, held.at[me], out_sems.at[0, 0, chips])
    mine.start()
    mine.wait()
    pl.semaphore_wait(barrier, 4)

    start(0, me, 1 - core).start()
    start(1, me, core).start()
    other = chip * 2 + 1 - core
    start(0, other, core).wait_recv()
    for kind in (0, 1):
        for d in (0, 1):
            ring(d, kind, 0, chip).start()
    start(1, other, 1 - core).wait_recv()

    def product(of, which):
        cols = span(which * quarter, quarter)
        return jnp.dot(
            normed_ref[of * 2], held[of * 2, :, cols], preferred_element_type=jnp.float32
        ) + jnp.dot(
            normed_ref[of * 2 + 1], held[of * 2 + 1, :, cols], preferred_element_type=jnp.float32
        )

    def write(of, which, index):
        at = (rows(of), slice(None), span(which * quarter, quarter))
        return pltpu.make_async_copy(
            held.at[at], whole_ref.at[at], out_sems.at[which // 2, lax.rem(which, 2), index]
        )

    def own(which, carry):
        write(chip, which, chips - 1).start()
        total[:, span(which * quarter, quarter)] = product(chip, which)
        return carry

    lax.fori_loop(0, 4, own, 0)

    def step(s, carry):
        @pl.when(s <= chips - 2)
        def _():
            for kind in (0, 1):
                for d in (0, 1):
                    ring(d, kind, s, arriving(d, s)).wait_recv()

                    @pl.when(s < chips - 2)
                    def _():
                        ring(d, kind, s + 1, arriving(d, s)).start()

                    pair(d, kind, s, core).start()
                    if kind == 1:
                        cross(d, 1, s).start()

        @pl.when((s >= 1) & (s <= chips - 1))
        def _():
            for d in (0, 1):
                cross(d, 2, s - 1).wait_recv()
                pair(d, 2, s - 1, core).start()

        @pl.when(s >= 2)
        def _():
            for d in (0, 1):
                for kind in (0, 1, 2):
                    pair(d, kind, s - 2, 1 - core).wait_recv()
                of = arriving(d, s - 2)
                for which in (d, 2 + d):
                    write(of, which, s - 2).start()
                    total[:, span(which * quarter, quarter)] += product(of, which)

        return carry

    lax.fori_loop(0, chips + 1, step, 0)
    keyval_ref[...] = total[...].astype(keyval_ref.dtype)

    start(0, me, 1 - core).wait_send()
    start(1, me, core).wait_send()

    def finish(s, carry):
        for d in (0, 1):
            for kind in (0, 1):
                ring(d, kind, s, leaving(d, s)).wait_send()
            for kind in (0, 1, 2):
                pair(d, kind, s, core).wait_send()
            cross(d, 1, s).wait_send()
            for which in (d, 2 + d):
                write(arriving(d, s), which, s).wait()
        return carry

    lax.fori_loop(0, chips - 1, finish, 0)
    for which in range(4):
        write(chip, which, chips - 1).wait()


def gather_project(kv_weight, normed):
    n = lax.axis_size("seq")
    chips = n // 2
    depth, doubled = kv_weight.shape
    tokens = normed.shape[0]
    parted = normed.reshape(tokens, n, depth).transpose(1, 0, 2)
    steps = chips - 1
    sems = pltpu.SemaphoreType.DMA
    whole, keyval = pl.pallas_call(
        functools.partial(gather_kernel, n),
        out_shape=(
            jax.ShapeDtypeStruct((n, depth, doubled), jnp.bfloat16),
            jax.ShapeDtypeStruct((tokens, doubled), jnp.bfloat16),
        ),
        in_specs=[
            pl.BlockSpec(memory_space=pl.ANY),
            pl.BlockSpec(memory_space=pltpu.VMEM),
        ],
        out_specs=(
            pl.BlockSpec(memory_space=pl.ANY),
            pl.BlockSpec(memory_space=pltpu.VMEM),
        ),
        scratch_shapes=[
            pltpu.VMEM((n, depth, doubled), jnp.bfloat16),
            pltpu.VMEM((tokens, doubled), jnp.float32),
            sems((2, 2, steps)),
            sems((2, 2, steps)),
            sems((2, 3, steps)),
            sems((2, 3, steps)),
            sems((2, steps)),
            sems((2, steps)),
            sems((2,)),
            sems((2,)),
            sems((2, 2, chips + 1)),
        ],
        compiler_params=pltpu.CompilerParams(
            collective_id=1, has_side_effects=True, vmem_limit_bytes=48 * 2**20
        ),
        name="gather_project",
    )(kv_weight, parted)
    return whole.reshape(n * depth, doubled), keyval


def shards(
    prefix,
    backbone_gain,
    kv_weight,
    lengths,
    assign,
    actions,
    flow_noise,
    timesteps,
    expert_gain,
    action_weight,
    query_weight,
    grad_attended,
):
    position = lax.axis_index("seq")
    owned_count, positions, model_width = prefix.shape
    episodes = assign.shape[0]
    doubled = kv_weight.shape[1]
    samples, horizon, q_width = (
        grad_attended.shape[1],
        grad_attended.shape[2],
        grad_attended.shape[3],
    )
    prefix_f32 = prefix.astype(jnp.float32)
    inverse_rms = lax.rsqrt(jnp.mean(prefix_f32 * prefix_f32, axis=-1, keepdims=True) + 1e-06)
    normed = (
        (prefix_f32 * inverse_rms * backbone_gain)
        .astype(jnp.bfloat16)
        .reshape(owned_count * positions, model_width)
    )
    n = lax.axis_size("seq")
    fits = doubled // n == HEAD and kv_weight.shape[0] % 16 == 0
    if fits and n % 4 == 0 and lax.axis_size("parts") == 2:
        whole_weight, product = gather_project(kv_weight, normed)
    else:
        whole_weight = lax.all_gather(kv_weight, "seq", axis=0, tiled=True)
        product = jnp.dot(normed, whole_weight, preferred_element_type=jnp.float32)
    keyval = product.astype(jnp.bfloat16).reshape(owned_count, positions, doubled)
    queries = expert_queries(
        actions, flow_noise, timesteps, expert_gain, action_weight, query_weight, HEAD
    )
    upstream = grad_attended.reshape(owned_count, samples * horizon, q_width)
    slot_index = jnp.arange(episodes, dtype=jnp.int32)
    matches = assign[None, :] == slot_index[:, None]
    inverse = jnp.sum(jnp.where(matches, slot_index[None, :], 0), axis=1)
    my_slots = lax.dynamic_slice_in_dim(assign, position * owned_count, owned_count)
    chosen = slot_index[None, :] == my_slots[:, None]
    owned_len = jnp.sum(jnp.where(chosen, lengths[None, :], 0), axis=1)
    if doubled // n == HEAD:
        row_count = samples * horizon
        extra = ((0, 0), (0, positions - row_count), (0, 0))
        attended, grad_query, grad_keyval = exchange(
            assign, inverse, owned_len, keyval, jnp.pad(queries, extra), jnp.pad(upstream, extra)
        )
        attended, grad_query = attended[:, :row_count], grad_query[:, :row_count]
    else:
        owned_kv = route_keys(keyval, assign)
        attended, grad_kv, grad_query = attend(queries, owned_kv, owned_len, upstream, KV_HEADS)
        grad_keyval = route_keys(grad_kv, inverse)
    restored = grad_keyval.reshape(owned_count * positions, doubled)
    grad_normed = lax.dot_general(
        restored, whole_weight, (((1,), (1,)), ((), ())), preferred_element_type=jnp.float32
    )
    gated = grad_normed.reshape(owned_count, positions, model_width) * backbone_gain
    grad_prefix = (
        inverse_rms * gated
        - prefix_f32 * inverse_rms**3 * jnp.mean(prefix_f32 * gated, axis=-1, keepdims=True)
    ).astype(jnp.bfloat16)
    shape_out = (owned_count, samples, horizon, q_width)
    return (attended.reshape(shape_out), grad_prefix, grad_query.reshape(shape_out))


def solution(mesh):
    placed = (
        P(("parts", "seq"), None, None),
        P(),
        P("seq", None),
        P("parts"),
        P("parts"),
        P(("parts", "seq"), None, None, None),
        P(("parts", "seq"), None, None, None),
        P(("parts", "seq"), None),
        P(),
        P(),
        P(),
        P(("parts", "seq"), None, None, None),
    )
    return jax.shard_map(
        shards,
        mesh=mesh,
        in_specs=placed,
        out_specs=(
            P(("parts", "seq"), None, None, None),
            P(("parts", "seq"), None, None),
            P(("parts", "seq"), None, None, None),
        ),
        check_vma=False,
    )
```

```python
import functools
import math

import jax
import jax.numpy as jnp
from jax import lax
from jax.experimental import pallas as pl
from jax.experimental.pallas import tpu as pltpu
from jax.sharding import PartitionSpec as P

KV_HEADS = 8
HEAD = 128


def time_features(times_in, model_width):
    half_width = model_width // 2
    ladder = jnp.arange(half_width, dtype=jnp.float32)
    frequency = jnp.exp(-math.log(10000.0) * ladder / half_width)
    angles = times_in[:, None] * 1000.0 * frequency[None, :]
    return jnp.concatenate([jnp.sin(angles), jnp.cos(angles)], axis=-1)


def expert_rows(actions, flow_noise, times_in, expert_gain, action_weight):
    batch_count, samples, horizon, action_dim = actions.shape
    model_width = action_weight.shape[1]
    flat_times = times_in.reshape(batch_count * samples)
    mixing = flat_times[:, None, None]
    noisy_actions = mixing * flow_noise.reshape(batch_count * samples, horizon, action_dim) + (
        1.0 - mixing
    ) * actions.reshape(batch_count * samples, horizon, action_dim)
    embedded = jnp.dot(
        noisy_actions.reshape(-1, action_dim).astype(jnp.bfloat16),
        action_weight,
        preferred_element_type=jnp.float32,
    )
    hidden = (
        embedded.reshape(batch_count * samples, horizon, model_width)
        + time_features(flat_times, model_width)[:, None, :]
    )
    inverse_rms = lax.rsqrt(jnp.mean(hidden * hidden, axis=-1, keepdims=True) + 1e-06)
    normed = (hidden * inverse_rms * expert_gain).astype(jnp.bfloat16)
    return normed.reshape(batch_count, samples * horizon, model_width)


def project_queries(normed, query_weight, head_dim):
    flat = normed.reshape(-1, normed.shape[-1])
    queries = (
        jnp.dot(flat, query_weight, preferred_element_type=jnp.float32) * head_dim ** (-0.5)
    ).astype(jnp.bfloat16)
    return queries.reshape(normed.shape[0], normed.shape[1], query_weight.shape[1])


def attend(queries, keyval, length, upstream, kv_heads):
    batch_count, row_count, q_width = queries.shape
    positions = keyval.shape[1]
    kv_width = keyval.shape[2] // 2
    head_dim = kv_width // kv_heads
    group_size = q_width // kv_width
    score_scale = head_dim ** (-0.5)
    query_heads = queries.reshape(batch_count, row_count, kv_heads, group_size, head_dim)
    key_rows = keyval[:, :, :kv_width].reshape(batch_count, positions, kv_heads, head_dim)
    value_rows = keyval[:, :, kv_width:].reshape(batch_count, positions, kv_heads, head_dim)
    scores = jnp.einsum(
        "bakgd,blkd->bkgal", query_heads, key_rows, preferred_element_type=jnp.float32
    )
    visible = (jnp.arange(positions, dtype=jnp.int32)[None, :] < length[:, None])[
        :, None, None, None, :
    ]
    masked = jnp.where(visible, scores, -1e30)
    row_top = jnp.max(masked, axis=-1, keepdims=True)
    exps = jnp.where(visible, jnp.exp(masked - row_top), 0.0)
    probabilities = exps / jnp.sum(exps, axis=-1, keepdims=True)
    rounded = probabilities.astype(jnp.bfloat16)
    attended = (
        jnp.einsum("bkgal,blkd->bakgd", rounded, value_rows, preferred_element_type=jnp.float32)
        .astype(jnp.bfloat16)
        .reshape(batch_count, row_count, q_width)
    )
    upstream_heads = upstream.reshape(batch_count, row_count, kv_heads, group_size, head_dim)
    grad_prob = jnp.einsum(
        "bakgd,blkd->bkgal", upstream_heads, value_rows, preferred_element_type=jnp.float32
    )
    grad_value = jnp.einsum(
        "bkgal,bakgd->blkd", rounded, upstream_heads, preferred_element_type=jnp.float32
    )
    grad_score = (
        probabilities * (grad_prob - jnp.sum(grad_prob * probabilities, axis=-1, keepdims=True))
    ).astype(jnp.bfloat16)
    grad_query = (
        (
            jnp.einsum(
                "bkgal,blkd->bakgd", grad_score, key_rows, preferred_element_type=jnp.float32
            )
            * score_scale
        )
        .astype(jnp.bfloat16)
        .reshape(batch_count, row_count, q_width)
    )
    grad_key = jnp.einsum(
        "bkgal,bakgd->blkd", grad_score, query_heads, preferred_element_type=jnp.float32
    )
    grad_kv = jnp.concatenate(
        [
            grad_key.reshape(batch_count, positions, kv_width),
            grad_value.reshape(batch_count, positions, kv_width),
        ],
        axis=-1,
    ).astype(jnp.bfloat16)
    return (attended, grad_kv, grad_query)


def route_keys(block, ordering):
    spread = lax.all_to_all(block, "seq", split_axis=2, concat_axis=0, tiled=True)
    arranged = jnp.take(spread, ordering, axis=0)
    return lax.all_to_all(arranged, "seq", split_axis=0, concat_axis=2, tiled=True)


def exchange_kernel(
    n,
    order_ref,
    inverse_ref,
    length_ref,
    keyval_ref,
    query_ref,
    upstream_ref,
    attended_ref,
    grad_query_ref,
    restored_ref,
    owned,
    spread,
    arranged,
    grads,
    spread_back,
    arranged_back,
    send_sems,
    recv_sems,
    local_sems,
):
    me = lax.axis_index("seq")
    own = keyval_ref.shape[0]
    heads = KV_HEADS
    episodes = spread.shape[0]

    def columns(index):
        return pl.ds(pl.multiple_of(index * HEAD, HEAD), HEAD)

    def rows(index):
        return pl.ds(index * own, own)

    def remote(stage, source, target, device, origin):
        return pltpu.make_async_remote_copy(
            src_ref=source,
            dst_ref=target,
            send_sem=send_sems.at[stage, device],
            recv_sem=recv_sems.at[stage, origin],
            device_id={"seq": device},
            device_id_type=pl.DeviceIdType.MESH,
        )

    def others(body):
        def step(k, carry):
            body(lax.rem(me + k, n))
            return carry

        lax.fori_loop(1, n, step, 0)

    barrier = pltpu.get_barrier_semaphore()
    others(
        lambda d: pl.semaphore_signal(
            barrier, inc=1, device_id={"seq": d}, device_id_type=pl.DeviceIdType.MESH
        )
    )
    pl.semaphore_wait(barrier, n - 1)

    def first(d):
        return remote(0, keyval_ref.at[:, :, columns(d)], spread.at[rows(me)], d, me)

    def first_in(d):
        return remote(0, keyval_ref.at[:, :, columns(d)], spread.at[rows(d)], d, d)

    kept = pltpu.make_async_copy(
        keyval_ref.at[:, :, columns(me)], spread.at[rows(me)], local_sems.at[0]
    )
    kept.start()
    others(lambda d: first(d).start())
    kept.wait()
    others(lambda d: first_in(d).wait_recv())

    def arrange(source, target, order):
        def step(e, carry):
            target[e] = source[order[e]]
            return carry

        lax.fori_loop(0, episodes, step, 0)

    arrange(spread, arranged, order_ref)

    def second(d):
        return remote(1, arranged.at[rows(d)], owned.at[:, :, columns(me)], d, me)

    def second_in(d):
        return remote(1, arranged.at[rows(d)], owned.at[:, :, columns(d)], d, d)

    kept = pltpu.make_async_copy(
        arranged.at[rows(me)], owned.at[:, :, columns(me)], local_sems.at[1]
    )
    kept.start()
    others(lambda d: second(d).start())
    kept.wait()

    def third(d):
        return remote(2, grads.at[:, :, columns(d)], spread_back.at[rows(me)], d, me)

    def third_in(d):
        return remote(2, grads.at[:, :, columns(d)], spread_back.at[rows(d)], d, d)

    def head(h, carry):
        for d in (h, h + heads):
            @pl.when(d != me)
            def _():
                second_in(d).wait_recv()

        even, odd = columns(2 * h), columns(2 * h + 1)
        for s in range(own):
            keys = owned[s, :, columns(h)]
            values = owned[s, :, columns(h + heads)]
            query = jnp.concatenate([query_ref[s, :, even], query_ref[s, :, odd]], axis=0)
            upstream = jnp.concatenate(
                [upstream_ref[s, :, even], upstream_ref[s, :, odd]], axis=0
            )
            half = query.shape[0] // 2
            scores = lax.dot_general(
                query, keys, (((1,), (1,)), ((), ())), preferred_element_type=jnp.float32
            )
            visible = lax.broadcasted_iota(jnp.int32, scores.shape, 1) < length_ref[s]
            masked = jnp.where(visible, scores, -1e30)
            exps = jnp.where(
                visible, jnp.exp(masked - jnp.max(masked, axis=-1, keepdims=True)), 0.0
            )
            probabilities = exps / jnp.sum(exps, axis=-1, keepdims=True)
            rounded = probabilities.astype(jnp.bfloat16)
            attended = jnp.dot(rounded, values, preferred_element_type=jnp.float32)
            grad_prob = lax.dot_general(
                upstream, values, (((1,), (1,)), ((), ())), preferred_element_type=jnp.float32
            )
            grad_value = lax.dot_general(
                rounded, upstream, (((0,), (0,)), ((), ())), preferred_element_type=jnp.float32
            )
            grad_score = (
                probabilities
                * (grad_prob - jnp.sum(grad_prob * probabilities, axis=-1, keepdims=True))
            ).astype(jnp.bfloat16)
            grad_query = (
                jnp.dot(grad_score, keys, preferred_element_type=jnp.float32) * HEAD ** (-0.5)
            )
            grad_key = lax.dot_general(
                grad_score, query, (((0,), (0,)), ((), ())), preferred_element_type=jnp.float32
            )
            attended_ref[s, :, even] = attended[:half].astype(jnp.bfloat16)
            attended_ref[s, :, odd] = attended[half:].astype(jnp.bfloat16)
            grad_query_ref[s, :, even] = grad_query[:half].astype(jnp.bfloat16)
            grad_query_ref[s, :, odd] = grad_query[half:].astype(jnp.bfloat16)
            grads[s, :, columns(h)] = grad_key.astype(jnp.bfloat16)
            grads[s, :, columns(h + heads)] = grad_value.astype(jnp.bfloat16)
        for d in (h, h + heads):
            @pl.when(d != me)
            def _():
                third(d).start()
        return carry

    lax.fori_loop(0, heads, head, 0)

    kept = pltpu.make_async_copy(
        grads.at[:, :, columns(me)], spread_back.at[rows(me)], local_sems.at[2]
    )
    kept.start()
    kept.wait()
    others(lambda d: third_in(d).wait_recv())
    arrange(spread_back, arranged_back, inverse_ref)

    def fourth(d):
        return remote(3, arranged_back.at[rows(d)], restored_ref.at[:, :, columns(me)], d, me)

    def fourth_in(d):
        return remote(3, arranged_back.at[rows(d)], restored_ref.at[:, :, columns(d)], d, d)

    kept = pltpu.make_async_copy(
        arranged_back.at[rows(me)], restored_ref.at[:, :, columns(me)], local_sems.at[3]
    )
    kept.start()
    others(lambda d: fourth(d).start())
    kept.wait()
    others(lambda d: fourth_in(d).wait_recv())

    def sent(d):
        first(d).wait_send()
        second(d).wait_send()
        third(d).wait_send()
        fourth(d).wait_send()

    others(sent)


def exchange(assign, inverse, owned_len, keyval, queries, upstream):
    n = lax.axis_size("seq")
    owned_count, positions, doubled = keyval.shape
    episodes = assign.shape[0]
    padded = jax.ShapeDtypeStruct(queries.shape, jnp.bfloat16)
    blocks = pltpu.VMEM((episodes, positions, HEAD), jnp.bfloat16)
    whole = pltpu.VMEM(keyval.shape, jnp.bfloat16)
    memory = pl.BlockSpec(memory_space=pltpu.VMEM)
    scalars = pl.BlockSpec(memory_space=pltpu.SMEM)
    return pl.pallas_call(
        functools.partial(exchange_kernel, n),
        out_shape=(padded, padded, jax.ShapeDtypeStruct(keyval.shape, jnp.bfloat16)),
        in_specs=[scalars] * 3 + [memory] * 3,
        out_specs=(memory,) * 3,
        scratch_shapes=[
            whole,
            blocks,
            blocks,
            whole,
            blocks,
            blocks,
            pltpu.SemaphoreType.DMA((4, n)),
            pltpu.SemaphoreType.DMA((4, n)),
            pltpu.SemaphoreType.DMA((4,)),
        ],
        compiler_params=pltpu.CompilerParams(
            collective_id=0, has_side_effects=True, vmem_limit_bytes=40 * 2**20
        ),
        name="exchange",
    )(assign, inverse, owned_len, keyval, queries, upstream)


def gather_kernel(
    n,
    weight_ref,
    tokens_ref,
    expert_ref,
    query_weight_ref,
    whole_ref,
    keyval_ref,
    queries_ref,
    normed_ref,
    held,
    total,
    ring_send,
    ring_recv,
    pair_send,
    pair_recv,
    cross_send,
    cross_recv,
    start_send,
    start_recv,
    out_sems,
):
    chips = n // 2
    part = lax.axis_index("parts")
    me = lax.axis_index("seq")
    chip, core = me // 2, lax.rem(me, 2)
    depth_place, side = chip // 2, lax.rem(chip, 2)
    place = depth_place + side * (chips - 1 - 2 * depth_place)
    width = held.shape[2]
    quarter, half, piece = width // 4, width // 2, width // 16

    def chip_at(position):
        position = lax.rem(position + 2 * chips, chips)
        return jnp.where(position < chips // 2, 2 * position, 2 * (chips - 1 - position) + 1)

    def span(start, size):
        return pl.ds(pl.multiple_of(start, piece), size)

    def columns(which, kind):
        if kind == 0:
            return span(which * quarter, 2 * piece)
        own = part if kind == 1 else 1 - part
        return span(which * quarter + (2 + own) * piece, piece)

    def rows(of):
        return pl.ds(of * 2, 2)

    def arriving(d, s):
        return chip_at(place - 1 - s if d == 0 else place + 1 + s)

    def leaving(d, s):
        return chip_at(place - s if d == 0 else place + s)

    def send(ref, device, send_sem, recv_sem):
        return pltpu.make_async_remote_copy(
            src_ref=ref,
            dst_ref=ref,
            send_sem=send_sem,
            recv_sem=recv_sem,
            device_id=device,
            device_id_type=pl.DeviceIdType.MESH,
        )

    onward = [{"seq": chip_at(place + 1) * 2 + core}, {"seq": chip_at(place - 1) * 2 + core}]
    sibling = {"seq": chip * 2 + 1 - core}
    opposite = {"parts": 1 - part, "seq": me}

    def ring(d, kind, s, of):
        ref = held.at[rows(of), :, columns(core * 2 + d, kind)]
        return send(ref, onward[d], ring_send.at[d, kind, s], ring_recv.at[d, kind, s])

    def pair(d, kind, s, whose):
        ref = held.at[rows(arriving(d, s)), :, columns(whose * 2 + d, kind)]
        return send(ref, sibling, pair_send.at[d, kind, s], pair_recv.at[d, kind, s])

    def cross(d, kind, s):
        ref = held.at[rows(arriving(d, s)), :, columns(core * 2 + d, kind)]
        return send(ref, opposite, cross_send.at[d, s], cross_recv.at[d, s])

    def start(k, shard, whose):
        ref = held.at[shard, :, span(whose * half, half)]
        return send(ref, sibling, start_send.at[k], start_recv.at[k])

    barrier = pltpu.get_barrier_semaphore()
    for device in (*onward, sibling, opposite):
        pl.semaphore_signal(
            barrier, inc=1, device_id=device, device_id_type=pl.DeviceIdType.MESH
        )
    mine = pltpu.make_async_copy(weight_ref, held.at[me], out_sems.at[0, 0, chips])
    mine.start()
    mine.wait()
    pl.semaphore_wait(barrier, 4)

    start(0, me, 1 - core).start()
    start(1, me, core).start()
    other = chip * 2 + 1 - core
    start(0, other, core).wait_recv()
    for kind in (0, 1):
        for d in (0, 1):
            ring(d, kind, 0, chip).start()
    depth = normed_ref.shape[2]
    for shard in range(n):
        normed_ref[shard] = tokens_ref[:, shard * depth : (shard + 1) * depth]
    start(1, other, 1 - core).wait_recv()

    def product(of, which):
        cols = span(which * quarter, quarter)
        return jnp.dot(
            normed_ref[of * 2], held[of * 2, :, cols], preferred_element_type=jnp.float32
        ) + jnp.dot(
            normed_ref[of * 2 + 1], held[of * 2 + 1, :, cols], preferred_element_type=jnp.float32
        )

    def write(of, which, index):
        at = (rows(of), slice(None), span(which * quarter, quarter))
        return pltpu.make_async_copy(
            held.at[at], whole_ref.at[at], out_sems.at[which // 2, lax.rem(which, 2), index]
        )

    def own(which, carry):
        write(chip, which, chips - 1).start()
        total[:, span(which * quarter, quarter)] = product(chip, which)
        return carry

    lax.fori_loop(0, 4, own, 0)

    def query(which, carry):
        cols = span(which * quarter, quarter)
        product_in = jnp.dot(
            expert_ref[...], query_weight_ref[:, cols], preferred_element_type=jnp.float32
        )
        queries_ref[:, cols] = (product_in * HEAD ** (-0.5)).astype(queries_ref.dtype)
        return carry

    lax.fori_loop(0, query_weight_ref.shape[1] // quarter, query, 0)

    def step(s, carry):
        @pl.when(s <= chips - 2)
        def _():
            for kind in (0, 1):
                for d in (0, 1):
                    ring(d, kind, s, arriving(d, s)).wait_recv()

                    @pl.when(s < chips - 2)
                    def _():
                        ring(d, kind, s + 1, arriving(d, s)).start()

                    pair(d, kind, s, core).start()
                    if kind == 1:
                        cross(d, 1, s).start()

        @pl.when((s >= 1) & (s <= chips - 1))
        def _():
            for d in (0, 1):
                cross(d, 2, s - 1).wait_recv()
                pair(d, 2, s - 1, core).start()

        @pl.when(s >= 2)
        def _():
            for d in (0, 1):
                for kind in (0, 1, 2):
                    pair(d, kind, s - 2, 1 - core).wait_recv()
                of = arriving(d, s - 2)
                for which in (d, 2 + d):
                    write(of, which, s - 2).start()
                    total[:, span(which * quarter, quarter)] += product(of, which)

        return carry

    lax.fori_loop(0, chips + 1, step, 0)
    keyval_ref[...] = total[...].astype(keyval_ref.dtype)

    start(0, me, 1 - core).wait_send()
    start(1, me, core).wait_send()

    def finish(s, carry):
        for d in (0, 1):
            for kind in (0, 1):
                ring(d, kind, s, leaving(d, s)).wait_send()
            for kind in (0, 1, 2):
                pair(d, kind, s, core).wait_send()
            cross(d, 1, s).wait_send()
            for which in (d, 2 + d):
                write(arriving(d, s), which, s).wait()
        return carry

    lax.fori_loop(0, chips - 1, finish, 0)
    for which in range(4):
        write(chip, which, chips - 1).wait()


def gather_project(kv_weight, normed, expert_normed, query_weight):
    n = lax.axis_size("seq")
    chips = n // 2
    depth, doubled = kv_weight.shape
    tokens = normed.shape[0]
    steps = chips - 1
    sems = pltpu.SemaphoreType.DMA
    whole, keyval, queries = pl.pallas_call(
        functools.partial(gather_kernel, n),
        out_shape=(
            jax.ShapeDtypeStruct((n, depth, doubled), jnp.bfloat16),
            jax.ShapeDtypeStruct((tokens, doubled), jnp.bfloat16),
            jax.ShapeDtypeStruct(
                (expert_normed.shape[0], query_weight.shape[1]), jnp.bfloat16
            ),
        ),
        in_specs=[
            pl.BlockSpec(memory_space=pl.ANY),
            pl.BlockSpec(memory_space=pltpu.VMEM),
            pl.BlockSpec(memory_space=pltpu.VMEM),
            pl.BlockSpec(memory_space=pltpu.VMEM),
        ],
        out_specs=(
            pl.BlockSpec(memory_space=pl.ANY),
            pl.BlockSpec(memory_space=pltpu.VMEM),
            pl.BlockSpec(memory_space=pltpu.VMEM),
        ),
        scratch_shapes=[
            pltpu.VMEM((n, tokens, depth), jnp.bfloat16),
            pltpu.VMEM((n, depth, doubled), jnp.bfloat16),
            pltpu.VMEM((tokens, doubled), jnp.float32),
            sems((2, 2, steps)),
            sems((2, 2, steps)),
            sems((2, 3, steps)),
            sems((2, 3, steps)),
            sems((2, steps)),
            sems((2, steps)),
            sems((2,)),
            sems((2,)),
            sems((2, 2, chips + 1)),
        ],
        compiler_params=pltpu.CompilerParams(
            collective_id=1, has_side_effects=True, vmem_limit_bytes=54 * 2**20
        ),
        name="gather_project",
    )(kv_weight, normed, expert_normed, query_weight)
    return whole.reshape(n * depth, doubled), keyval, queries


def shards(
    prefix,
    backbone_gain,
    kv_weight,
    lengths,
    assign,
    actions,
    flow_noise,
    timesteps,
    expert_gain,
    action_weight,
    query_weight,
    grad_attended,
):
    position = lax.axis_index("seq")
    owned_count, positions, model_width = prefix.shape
    episodes = assign.shape[0]
    doubled = kv_weight.shape[1]
    samples, horizon, q_width = (
        grad_attended.shape[1],
        grad_attended.shape[2],
        grad_attended.shape[3],
    )
    prefix_f32 = prefix.astype(jnp.float32)
    inverse_rms = lax.rsqrt(jnp.mean(prefix_f32 * prefix_f32, axis=-1, keepdims=True) + 1e-06)
    normed = (
        (prefix_f32 * inverse_rms * backbone_gain)
        .astype(jnp.bfloat16)
        .reshape(owned_count * positions, model_width)
    )
    n = lax.axis_size("seq")
    fits = doubled // n == HEAD and kv_weight.shape[0] % 16 == 0
    fits = fits and n % 4 == 0 and lax.axis_size("parts") == 2
    row_count = samples * horizon
    extra = ((0, 0), (0, positions - row_count), (0, 0))
    expert = expert_rows(actions, flow_noise, timesteps, expert_gain, action_weight)
    if fits:
        flat = jnp.pad(expert, extra).reshape(owned_count * positions, expert.shape[-1])
        whole_weight, product, queries = gather_project(kv_weight, normed, flat, query_weight)
        queries = queries.reshape(owned_count, positions, q_width)
    else:
        whole_weight = lax.all_gather(kv_weight, "seq", axis=0, tiled=True)
        product = jnp.dot(normed, whole_weight, preferred_element_type=jnp.float32)
        queries = project_queries(expert, query_weight, HEAD)
    keyval = product.astype(jnp.bfloat16).reshape(owned_count, positions, doubled)
    upstream = grad_attended.reshape(owned_count, samples * horizon, q_width)
    slot_index = jnp.arange(episodes, dtype=jnp.int32)
    matches = assign[None, :] == slot_index[:, None]
    inverse = jnp.sum(jnp.where(matches, slot_index[None, :], 0), axis=1)
    my_slots = lax.dynamic_slice_in_dim(assign, position * owned_count, owned_count)
    chosen = slot_index[None, :] == my_slots[:, None]
    owned_len = jnp.sum(jnp.where(chosen, lengths[None, :], 0), axis=1)
    if fits:
        attended, grad_query, grad_keyval = exchange(
            assign, inverse, owned_len, keyval, queries, jnp.pad(upstream, extra)
        )
        attended, grad_query = attended[:, :row_count], grad_query[:, :row_count]
    else:
        owned_kv = route_keys(keyval, assign)
        attended, grad_kv, grad_query = attend(queries, owned_kv, owned_len, upstream, KV_HEADS)
        grad_keyval = route_keys(grad_kv, inverse)
    restored = grad_keyval.reshape(owned_count * positions, doubled)
    grad_normed = lax.dot_general(
        restored, whole_weight, (((1,), (1,)), ((), ())), preferred_element_type=jnp.float32
    )
    gated = grad_normed.reshape(owned_count, positions, model_width) * backbone_gain
    grad_prefix = (
        inverse_rms * gated
        - prefix_f32 * inverse_rms**3 * jnp.mean(prefix_f32 * gated, axis=-1, keepdims=True)
    ).astype(jnp.bfloat16)
    shape_out = (owned_count, samples, horizon, q_width)
    return (attended.reshape(shape_out), grad_prefix, grad_query.reshape(shape_out))


def solution(mesh):
    placed = (
        P(("parts", "seq"), None, None),
        P(),
        P("seq", None),
        P("parts"),
        P("parts"),
        P(("parts", "seq"), None, None, None),
        P(("parts", "seq"), None, None, None),
        P(("parts", "seq"), None),
        P(),
        P(),
        P(),
        P(("parts", "seq"), None, None, None),
    )
    return jax.shard_map(
        shards,
        mesh=mesh,
        in_specs=placed,
        out_specs=(
            P(("parts", "seq"), None, None, None),
            P(("parts", "seq"), None, None),
            P(("parts", "seq"), None, None, None),
        ),
        check_vma=False,
    )
```

```python
import functools
import math

import jax
import jax.numpy as jnp
from jax import lax
from jax.experimental import pallas as pl
from jax.experimental.pallas import tpu as pltpu
from jax.sharding import PartitionSpec as P

KV_HEADS = 8
HEAD = 128


def time_features(times_in, model_width):
    half_width = model_width // 2
    ladder = jnp.arange(half_width, dtype=jnp.float32)
    frequency = jnp.exp(-math.log(10000.0) * ladder / half_width)
    angles = times_in[:, None] * 1000.0 * frequency[None, :]
    return jnp.concatenate([jnp.sin(angles), jnp.cos(angles)], axis=-1)


def expert_rows(actions, flow_noise, times_in, expert_gain, action_weight):
    batch_count, samples, horizon, action_dim = actions.shape
    model_width = action_weight.shape[1]
    flat_times = times_in.reshape(batch_count * samples)
    mixing = flat_times[:, None, None]
    noisy_actions = mixing * flow_noise.reshape(batch_count * samples, horizon, action_dim) + (
        1.0 - mixing
    ) * actions.reshape(batch_count * samples, horizon, action_dim)
    embedded = jnp.dot(
        noisy_actions.reshape(-1, action_dim).astype(jnp.bfloat16),
        action_weight,
        preferred_element_type=jnp.float32,
    )
    hidden = (
        embedded.reshape(batch_count * samples, horizon, model_width)
        + time_features(flat_times, model_width)[:, None, :]
    )
    inverse_rms = lax.rsqrt(jnp.mean(hidden * hidden, axis=-1, keepdims=True) + 1e-06)
    normed = (hidden * inverse_rms * expert_gain).astype(jnp.bfloat16)
    return normed.reshape(batch_count, samples * horizon, model_width)


def project_queries(normed, query_weight, head_dim):
    flat = normed.reshape(-1, normed.shape[-1])
    queries = (
        jnp.dot(flat, query_weight, preferred_element_type=jnp.float32) * head_dim ** (-0.5)
    ).astype(jnp.bfloat16)
    return queries.reshape(normed.shape[0], normed.shape[1], query_weight.shape[1])


def attend(queries, keyval, length, upstream, kv_heads):
    batch_count, row_count, q_width = queries.shape
    positions = keyval.shape[1]
    kv_width = keyval.shape[2] // 2
    head_dim = kv_width // kv_heads
    group_size = q_width // kv_width
    score_scale = head_dim ** (-0.5)
    query_heads = queries.reshape(batch_count, row_count, kv_heads, group_size, head_dim)
    key_rows = keyval[:, :, :kv_width].reshape(batch_count, positions, kv_heads, head_dim)
    value_rows = keyval[:, :, kv_width:].reshape(batch_count, positions, kv_heads, head_dim)
    scores = jnp.einsum(
        "bakgd,blkd->bkgal", query_heads, key_rows, preferred_element_type=jnp.float32
    )
    visible = (jnp.arange(positions, dtype=jnp.int32)[None, :] < length[:, None])[
        :, None, None, None, :
    ]
    masked = jnp.where(visible, scores, -1e30)
    row_top = jnp.max(masked, axis=-1, keepdims=True)
    exps = jnp.where(visible, jnp.exp(masked - row_top), 0.0)
    probabilities = exps / jnp.sum(exps, axis=-1, keepdims=True)
    rounded = probabilities.astype(jnp.bfloat16)
    attended = (
        jnp.einsum("bkgal,blkd->bakgd", rounded, value_rows, preferred_element_type=jnp.float32)
        .astype(jnp.bfloat16)
        .reshape(batch_count, row_count, q_width)
    )
    upstream_heads = upstream.reshape(batch_count, row_count, kv_heads, group_size, head_dim)
    grad_prob = jnp.einsum(
        "bakgd,blkd->bkgal", upstream_heads, value_rows, preferred_element_type=jnp.float32
    )
    grad_value = jnp.einsum(
        "bkgal,bakgd->blkd", rounded, upstream_heads, preferred_element_type=jnp.float32
    )
    grad_score = (
        probabilities * (grad_prob - jnp.sum(grad_prob * probabilities, axis=-1, keepdims=True))
    ).astype(jnp.bfloat16)
    grad_query = (
        (
            jnp.einsum(
                "bkgal,blkd->bakgd", grad_score, key_rows, preferred_element_type=jnp.float32
            )
            * score_scale
        )
        .astype(jnp.bfloat16)
        .reshape(batch_count, row_count, q_width)
    )
    grad_key = jnp.einsum(
        "bkgal,bakgd->blkd", grad_score, query_heads, preferred_element_type=jnp.float32
    )
    grad_kv = jnp.concatenate(
        [
            grad_key.reshape(batch_count, positions, kv_width),
            grad_value.reshape(batch_count, positions, kv_width),
        ],
        axis=-1,
    ).astype(jnp.bfloat16)
    return (attended, grad_kv, grad_query)


def route_keys(block, ordering):
    spread = lax.all_to_all(block, "seq", split_axis=2, concat_axis=0, tiled=True)
    arranged = jnp.take(spread, ordering, axis=0)
    return lax.all_to_all(arranged, "seq", split_axis=0, concat_axis=2, tiled=True)


def exchange_kernel(
    n,
    order_ref,
    inverse_ref,
    length_ref,
    keyval_ref,
    query_ref,
    upstream_ref,
    attended_ref,
    grad_query_ref,
    restored_ref,
    owned,
    spread,
    arranged,
    grads,
    spread_back,
    arranged_back,
    send_sems,
    recv_sems,
    local_sems,
):
    me = lax.axis_index("seq")
    own = keyval_ref.shape[0]
    heads = KV_HEADS

    def columns(index):
        return pl.ds(pl.multiple_of(index * HEAD, HEAD), HEAD)

    def rows(index):
        return pl.ds(index * own, own)

    def remote(stage, source, target, device, origin):
        return pltpu.make_async_remote_copy(
            src_ref=source,
            dst_ref=target,
            send_sem=send_sems.at[stage, device],
            recv_sem=recv_sems.at[stage, origin],
            device_id={"seq": device},
            device_id_type=pl.DeviceIdType.MESH,
        )

    def others(body):
        def step(k, carry):
            body(lax.rem(me + k, n))
            return carry

        lax.fori_loop(1, n, step, 0)

    barrier = pltpu.get_barrier_semaphore()
    others(
        lambda d: pl.semaphore_signal(
            barrier, inc=1, device_id={"seq": d}, device_id_type=pl.DeviceIdType.MESH
        )
    )
    pl.semaphore_wait(barrier, n - 1)

    def first(d):
        return remote(0, keyval_ref.at[:, :, columns(d)], spread.at[rows(me)], d, me)

    def first_in(d):
        return remote(0, keyval_ref.at[:, :, columns(d)], spread.at[rows(d)], d, d)

    kept = pltpu.make_async_copy(
        keyval_ref.at[:, :, columns(me)], spread.at[rows(me)], local_sems.at[0]
    )
    kept.start()
    others(lambda d: first(d).start())
    kept.wait()
    others(lambda d: first_in(d).wait_recv())

    def arrange(source, target, order, d):
        for e in range(own):
            target[d * own + e] = source[order[d * own + e]]

    def second(d):
        return remote(1, arranged.at[rows(d)], owned.at[:, :, columns(me)], d, me)

    def second_in(d):
        return remote(1, arranged.at[rows(d)], owned.at[:, :, columns(d)], d, d)

    arrange(spread, arranged, order_ref, me)
    kept = pltpu.make_async_copy(
        arranged.at[rows(me)], owned.at[:, :, columns(me)], local_sems.at[1]
    )
    kept.start()

    def second_out(d):
        arrange(spread, arranged, order_ref, d)
        second(d).start()

    others(second_out)
    kept.wait()

    def third(d):
        return remote(2, grads.at[:, :, columns(d)], spread_back.at[rows(me)], d, me)

    def third_in(d):
        return remote(2, grads.at[:, :, columns(d)], spread_back.at[rows(d)], d, d)

    def head(h, carry):
        for d in (h, h + heads):
            @pl.when(d != me)
            def _():
                second_in(d).wait_recv()

        even, odd = columns(2 * h), columns(2 * h + 1)
        for s in range(own):
            keys = owned[s, :, columns(h)]
            values = owned[s, :, columns(h + heads)]
            query = jnp.concatenate([query_ref[s, :, even], query_ref[s, :, odd]], axis=0)
            upstream = jnp.concatenate(
                [upstream_ref[s, :, even], upstream_ref[s, :, odd]], axis=0
            )
            half = query.shape[0] // 2
            scores = lax.dot_general(
                query, keys, (((1,), (1,)), ((), ())), preferred_element_type=jnp.float32
            )
            visible = lax.broadcasted_iota(jnp.int32, scores.shape, 1) < length_ref[s]
            masked = jnp.where(visible, scores, -1e30)
            exps = jnp.where(
                visible, jnp.exp(masked - jnp.max(masked, axis=-1, keepdims=True)), 0.0
            )
            probabilities = exps / jnp.sum(exps, axis=-1, keepdims=True)
            rounded = probabilities.astype(jnp.bfloat16)
            attended = jnp.dot(rounded, values, preferred_element_type=jnp.float32)
            grad_prob = lax.dot_general(
                upstream, values, (((1,), (1,)), ((), ())), preferred_element_type=jnp.float32
            )
            grad_value = lax.dot_general(
                rounded, upstream, (((0,), (0,)), ((), ())), preferred_element_type=jnp.float32
            )
            grad_score = (
                probabilities
                * (grad_prob - jnp.sum(grad_prob * probabilities, axis=-1, keepdims=True))
            ).astype(jnp.bfloat16)
            grad_query = (
                jnp.dot(grad_score, keys, preferred_element_type=jnp.float32) * HEAD ** (-0.5)
            )
            grad_key = lax.dot_general(
                grad_score, query, (((0,), (0,)), ((), ())), preferred_element_type=jnp.float32
            )
            attended_ref[s, :, even] = attended[:half].astype(jnp.bfloat16)
            attended_ref[s, :, odd] = attended[half:].astype(jnp.bfloat16)
            grad_query_ref[s, :, even] = grad_query[:half].astype(jnp.bfloat16)
            grad_query_ref[s, :, odd] = grad_query[half:].astype(jnp.bfloat16)
            grads[s, :, columns(h)] = grad_key.astype(jnp.bfloat16)
            grads[s, :, columns(h + heads)] = grad_value.astype(jnp.bfloat16)
        for d in (h, h + heads):
            @pl.when(d != me)
            def _():
                third(d).start()
        return carry

    lax.fori_loop(0, heads, head, 0)

    kept = pltpu.make_async_copy(
        grads.at[:, :, columns(me)], spread_back.at[rows(me)], local_sems.at[2]
    )
    kept.start()
    kept.wait()
    others(lambda d: third_in(d).wait_recv())

    def fourth(d):
        return remote(3, arranged_back.at[rows(d)], restored_ref.at[:, :, columns(me)], d, me)

    def fourth_in(d):
        return remote(3, arranged_back.at[rows(d)], restored_ref.at[:, :, columns(d)], d, d)

    arrange(spread_back, arranged_back, inverse_ref, me)
    kept = pltpu.make_async_copy(
        arranged_back.at[rows(me)], restored_ref.at[:, :, columns(me)], local_sems.at[3]
    )
    kept.start()

    def fourth_out(d):
        arrange(spread_back, arranged_back, inverse_ref, d)
        fourth(d).start()

    others(fourth_out)
    kept.wait()
    others(lambda d: fourth_in(d).wait_recv())

    def sent(d):
        first(d).wait_send()
        second(d).wait_send()
        third(d).wait_send()
        fourth(d).wait_send()

    others(sent)


def exchange(assign, inverse, owned_len, keyval, queries, upstream):
    n = lax.axis_size("seq")
    owned_count, positions, doubled = keyval.shape
    episodes = assign.shape[0]
    padded = jax.ShapeDtypeStruct(queries.shape, jnp.bfloat16)
    blocks = pltpu.VMEM((episodes, positions, HEAD), jnp.bfloat16)
    whole = pltpu.VMEM(keyval.shape, jnp.bfloat16)
    memory = pl.BlockSpec(memory_space=pltpu.VMEM)
    scalars = pl.BlockSpec(memory_space=pltpu.SMEM)
    return pl.pallas_call(
        functools.partial(exchange_kernel, n),
        out_shape=(padded, padded, jax.ShapeDtypeStruct(keyval.shape, jnp.bfloat16)),
        in_specs=[scalars] * 3 + [memory] * 3,
        out_specs=(memory,) * 3,
        scratch_shapes=[
            whole,
            blocks,
            blocks,
            whole,
            blocks,
            blocks,
            pltpu.SemaphoreType.DMA((4, n)),
            pltpu.SemaphoreType.DMA((4, n)),
            pltpu.SemaphoreType.DMA((4,)),
        ],
        compiler_params=pltpu.CompilerParams(
            collective_id=0, has_side_effects=True, vmem_limit_bytes=40 * 2**20
        ),
        name="exchange",
    )(assign, inverse, owned_len, keyval, queries, upstream)


def gather_kernel(
    n,
    weight_ref,
    tokens_ref,
    expert_ref,
    query_weight_ref,
    whole_ref,
    keyval_ref,
    queries_ref,
    normed_ref,
    held,
    total,
    ring_send,
    ring_recv,
    pair_send,
    pair_recv,
    cross_send,
    cross_recv,
    start_send,
    start_recv,
    out_sems,
):
    chips = n // 2
    part = lax.axis_index("parts")
    me = lax.axis_index("seq")
    chip, core = me // 2, lax.rem(me, 2)
    depth_place, side = chip // 2, lax.rem(chip, 2)
    place = depth_place + side * (chips - 1 - 2 * depth_place)
    width = held.shape[2]
    quarter, half, piece = width // 4, width // 2, width // 16

    def chip_at(position):
        position = lax.rem(position + 2 * chips, chips)
        return jnp.where(position < chips // 2, 2 * position, 2 * (chips - 1 - position) + 1)

    def span(start, size):
        return pl.ds(pl.multiple_of(start, piece), size)

    def columns(which, kind):
        if kind == 0:
            return span(which * quarter, 2 * piece)
        own = part if kind == 1 else 1 - part
        return span(which * quarter + (2 + own) * piece, piece)

    def rows(of):
        return pl.ds(of * 2, 2)

    def arriving(d, s):
        return chip_at(place - 1 - s if d == 0 else place + 1 + s)

    def leaving(d, s):
        return chip_at(place - s if d == 0 else place + s)

    def send(ref, device, send_sem, recv_sem):
        return pltpu.make_async_remote_copy(
            src_ref=ref,
            dst_ref=ref,
            send_sem=send_sem,
            recv_sem=recv_sem,
            device_id=device,
            device_id_type=pl.DeviceIdType.MESH,
        )

    onward = [{"seq": chip_at(place + 1) * 2 + core}, {"seq": chip_at(place - 1) * 2 + core}]
    sibling = {"seq": chip * 2 + 1 - core}
    opposite = {"parts": 1 - part, "seq": me}

    def ring(d, kind, s, of):
        ref = held.at[rows(of), :, columns(core * 2 + d, kind)]
        return send(ref, onward[d], ring_send.at[d, kind, s], ring_recv.at[d, kind, s])

    def pair(d, kind, s, whose):
        ref = held.at[rows(arriving(d, s)), :, columns(whose * 2 + d, kind)]
        return send(ref, sibling, pair_send.at[d, kind, s], pair_recv.at[d, kind, s])

    def cross(d, kind, s):
        ref = held.at[rows(arriving(d, s)), :, columns(core * 2 + d, kind)]
        return send(ref, opposite, cross_send.at[d, s], cross_recv.at[d, s])

    def start(k, shard, whose):
        ref = held.at[shard, :, span(whose * half, half)]
        return send(ref, sibling, start_send.at[k], start_recv.at[k])

    barrier = pltpu.get_barrier_semaphore()
    for device in (*onward, sibling, opposite):
        pl.semaphore_signal(
            barrier, inc=1, device_id=device, device_id_type=pl.DeviceIdType.MESH
        )
    mine = pltpu.make_async_copy(weight_ref, held.at[me], out_sems.at[0, 0, chips])
    mine.start()
    mine.wait()
    pl.semaphore_wait(barrier, 4)

    start(0, me, 1 - core).start()
    start(1, me, core).start()
    other = chip * 2 + 1 - core
    start(0, other, core).wait_recv()
    for kind in (0, 1):
        for d in (0, 1):
            ring(d, kind, 0, chip).start()
    depth = normed_ref.shape[2]
    for shard in range(n):
        normed_ref[shard] = tokens_ref[:, shard * depth : (shard + 1) * depth]
    start(1, other, 1 - core).wait_recv()

    def product(of, which):
        cols = span(which * quarter, quarter)
        return jnp.dot(
            normed_ref[of * 2], held[of * 2, :, cols], preferred_element_type=jnp.float32
        ) + jnp.dot(
            normed_ref[of * 2 + 1], held[of * 2 + 1, :, cols], preferred_element_type=jnp.float32
        )

    def write(of, which, index):
        at = (rows(of), slice(None), span(which * quarter, quarter))
        return pltpu.make_async_copy(
            held.at[at], whole_ref.at[at], out_sems.at[which // 2, lax.rem(which, 2), index]
        )

    def own(which, carry):
        write(chip, which, chips - 1).start()
        total[:, span(which * quarter, quarter)] = product(chip, which)
        return carry

    lax.fori_loop(0, 4, own, 0)

    def query(which, carry):
        cols = span(which * quarter, quarter)
        product_in = jnp.dot(
            expert_ref[...], query_weight_ref[:, cols], preferred_element_type=jnp.float32
        )
        queries_ref[:, cols] = (product_in * HEAD ** (-0.5)).astype(queries_ref.dtype)
        return carry

    lax.fori_loop(0, query_weight_ref.shape[1] // quarter, query, 0)

    def step(s, carry):
        @pl.when(s <= chips - 2)
        def _():
            for kind in (0, 1):
                for d in (0, 1):
                    ring(d, kind, s, arriving(d, s)).wait_recv()

                    @pl.when(s < chips - 2)
                    def _():
                        ring(d, kind, s + 1, arriving(d, s)).start()

                    pair(d, kind, s, core).start()
                    if kind == 1:
                        cross(d, 1, s).start()

        @pl.when((s >= 1) & (s <= chips - 1))
        def _():
            for d in (0, 1):
                cross(d, 2, s - 1).wait_recv()
                pair(d, 2, s - 1, core).start()

        @pl.when(s >= 2)
        def _():
            for d in (0, 1):
                for kind in (0, 1, 2):
                    pair(d, kind, s - 2, 1 - core).wait_recv()
                of = arriving(d, s - 2)
                for which in (d, 2 + d):
                    write(of, which, s - 2).start()
                    total[:, span(which * quarter, quarter)] += product(of, which)

        return carry

    lax.fori_loop(0, chips + 1, step, 0)
    keyval_ref[...] = total[...].astype(keyval_ref.dtype)

    start(0, me, 1 - core).wait_send()
    start(1, me, core).wait_send()

    def finish(s, carry):
        for d in (0, 1):
            for kind in (0, 1):
                ring(d, kind, s, leaving(d, s)).wait_send()
            for kind in (0, 1, 2):
                pair(d, kind, s, core).wait_send()
            cross(d, 1, s).wait_send()
            for which in (d, 2 + d):
                write(arriving(d, s), which, s).wait()
        return carry

    lax.fori_loop(0, chips - 1, finish, 0)
    for which in range(4):
        write(chip, which, chips - 1).wait()


def gather_project(kv_weight, normed, expert_normed, query_weight):
    n = lax.axis_size("seq")
    chips = n // 2
    depth, doubled = kv_weight.shape
    tokens = normed.shape[0]
    steps = chips - 1
    sems = pltpu.SemaphoreType.DMA
    whole, keyval, queries = pl.pallas_call(
        functools.partial(gather_kernel, n),
        out_shape=(
            jax.ShapeDtypeStruct((n, depth, doubled), jnp.bfloat16),
            jax.ShapeDtypeStruct((tokens, doubled), jnp.bfloat16),
            jax.ShapeDtypeStruct(
                (expert_normed.shape[0], query_weight.shape[1]), jnp.bfloat16
            ),
        ),
        in_specs=[
            pl.BlockSpec(memory_space=pl.ANY),
            pl.BlockSpec(memory_space=pltpu.VMEM),
            pl.BlockSpec(memory_space=pltpu.VMEM),
            pl.BlockSpec(memory_space=pltpu.VMEM),
        ],
        out_specs=(
            pl.BlockSpec(memory_space=pl.ANY),
            pl.BlockSpec(memory_space=pltpu.VMEM),
            pl.BlockSpec(memory_space=pltpu.VMEM),
        ),
        scratch_shapes=[
            pltpu.VMEM((n, tokens, depth), jnp.bfloat16),
            pltpu.VMEM((n, depth, doubled), jnp.bfloat16),
            pltpu.VMEM((tokens, doubled), jnp.float32),
            sems((2, 2, steps)),
            sems((2, 2, steps)),
            sems((2, 3, steps)),
            sems((2, 3, steps)),
            sems((2, steps)),
            sems((2, steps)),
            sems((2,)),
            sems((2,)),
            sems((2, 2, chips + 1)),
        ],
        compiler_params=pltpu.CompilerParams(
            collective_id=1, has_side_effects=True, vmem_limit_bytes=54 * 2**20
        ),
        name="gather_project",
    )(kv_weight, normed, expert_normed, query_weight)
    return whole.reshape(n * depth, doubled), keyval, queries


def shards(
    prefix,
    backbone_gain,
    kv_weight,
    lengths,
    assign,
    actions,
    flow_noise,
    timesteps,
    expert_gain,
    action_weight,
    query_weight,
    grad_attended,
):
    position = lax.axis_index("seq")
    owned_count, positions, model_width = prefix.shape
    episodes = assign.shape[0]
    doubled = kv_weight.shape[1]
    samples, horizon, q_width = (
        grad_attended.shape[1],
        grad_attended.shape[2],
        grad_attended.shape[3],
    )
    prefix_f32 = prefix.astype(jnp.float32)
    inverse_rms = lax.rsqrt(jnp.mean(prefix_f32 * prefix_f32, axis=-1, keepdims=True) + 1e-06)
    normed = (
        (prefix_f32 * inverse_rms * backbone_gain)
        .astype(jnp.bfloat16)
        .reshape(owned_count * positions, model_width)
    )
    n = lax.axis_size("seq")
    fits = doubled // n == HEAD and kv_weight.shape[0] % 16 == 0
    fits = fits and n % 4 == 0 and lax.axis_size("parts") == 2
    row_count = samples * horizon
    extra = ((0, 0), (0, positions - row_count), (0, 0))
    expert = expert_rows(actions, flow_noise, timesteps, expert_gain, action_weight)
    if fits:
        flat = jnp.pad(expert, extra).reshape(owned_count * positions, expert.shape[-1])
        whole_weight, product, queries = gather_project(kv_weight, normed, flat, query_weight)
        queries = queries.reshape(owned_count, positions, q_width)
    else:
        whole_weight = lax.all_gather(kv_weight, "seq", axis=0, tiled=True)
        product = jnp.dot(normed, whole_weight, preferred_element_type=jnp.float32)
        queries = project_queries(expert, query_weight, HEAD)
    keyval = product.astype(jnp.bfloat16).reshape(owned_count, positions, doubled)
    upstream = grad_attended.reshape(owned_count, samples * horizon, q_width)
    slot_index = jnp.arange(episodes, dtype=jnp.int32)
    matches = assign[None, :] == slot_index[:, None]
    inverse = jnp.sum(jnp.where(matches, slot_index[None, :], 0), axis=1)
    my_slots = lax.dynamic_slice_in_dim(assign, position * owned_count, owned_count)
    chosen = slot_index[None, :] == my_slots[:, None]
    owned_len = jnp.sum(jnp.where(chosen, lengths[None, :], 0), axis=1)
    if fits:
        attended, grad_query, grad_keyval = exchange(
            assign, inverse, owned_len, keyval, queries, jnp.pad(upstream, extra)
        )
        attended, grad_query = attended[:, :row_count], grad_query[:, :row_count]
    else:
        owned_kv = route_keys(keyval, assign)
        attended, grad_kv, grad_query = attend(queries, owned_kv, owned_len, upstream, KV_HEADS)
        grad_keyval = route_keys(grad_kv, inverse)
    restored = grad_keyval.reshape(owned_count * positions, doubled)
    grad_normed = lax.dot_general(
        restored, whole_weight, (((1,), (1,)), ((), ())), preferred_element_type=jnp.float32
    )
    gated = grad_normed.reshape(owned_count, positions, model_width) * backbone_gain
    grad_prefix = (
        inverse_rms * gated
        - prefix_f32 * inverse_rms**3 * jnp.mean(prefix_f32 * gated, axis=-1, keepdims=True)
    ).astype(jnp.bfloat16)
    shape_out = (owned_count, samples, horizon, q_width)
    return (attended.reshape(shape_out), grad_prefix, grad_query.reshape(shape_out))


def solution(mesh):
    placed = (
        P(("parts", "seq"), None, None),
        P(),
        P("seq", None),
        P("parts"),
        P("parts"),
        P(("parts", "seq"), None, None, None),
        P(("parts", "seq"), None, None, None),
        P(("parts", "seq"), None),
        P(),
        P(),
        P(),
        P(("parts", "seq"), None, None, None),
    )
    return jax.shard_map(
        shards,
        mesh=mesh,
        in_specs=placed,
        out_specs=(
            P(("parts", "seq"), None, None, None),
            P(("parts", "seq"), None, None),
            P(("parts", "seq"), None, None, None),
        ),
        check_vma=False,
    )
```
